512 devices in a mesh: narrow: 16 (over z, core), wide: 32 (over x, y).
Axes of the slice: x: 4, y: 8, z: 8, core: 2. Of those that a mesh axis runs over, the one named last changes fastest.
Arguments:
- activations: bfloat16 [131072, 8192], P(('narrow', 'wide')), may hold values from -24 to 24
- out_grads: bfloat16 [131072, 512], P(('narrow', 'wide')), may hold values from -6 to 6
Outputs:
- mean_grad: float32 [8192, 512], P(('narrow', 'wide'))
The draws below stay inside these ranges and needn't reach their ends.
All inputs are finite; a program needn't handle non-finite values.
Results may differ from the reference program's by a relative error of at most 0.0065.
Values may be sent and summed in bfloat16 or wider, within the bound.
A program may use at most 128 MiB of HBM per device.

```python
import math
import jax
import jax.numpy as jnp
from jax import lax

D = 8192
COLS = 512
TOK_DEV = 256
BLOCK = 128
TOKENS = 131072
N_NARROW = 16
N_WIDE = 32


def with_spikes(result, rng, source, target, parts, factor):
    owner, partner = [(jnp.arange(result.shape[axis_at]) // (result.shape[axis_at] // parts)).reshape([-1 if axis == axis_at else 1 for axis in range(result.ndim)]) for axis_at in (source, target)]
    chosen = jax.random.permutation(rng, parts)[partner]
    strong = (owner == chosen) | (owner == (partner + parts // 2) % parts)
    return jnp.where(strong, factor * result, result)


def block_scale(key, extent, shards, least, high):
    gain, own = 1.0, jax.random.fold_in(key, 6)
    for dim, blocks in shards:
        heights = jnp.exp(jax.random.uniform(jax.random.fold_in(own, dim), (blocks,), jnp.float32, least / len(shards), high / len(shards)))
        gain = gain * jnp.repeat(heights, extent[dim] // blocks).reshape([-1 if axis == dim else 1 for axis in range(len(extent))])
    return gain


def bell_draw(key, shape, deviation, bound, pieces=(), held_as=jnp.bfloat16):
    drawn = deviation * jax.random.normal(key, shape, jnp.float32)
    if pieces:
        drawn = drawn * block_scale(key, shape, pieces, -0.22, 0.18)
    return jnp.clip(drawn, -bound, bound).astype(held_as)


def bell_draw_with(rng, dims, scale, limit, pieces, heavy, kind=jnp.bfloat16):
    array = scale * jax.random.normal(rng, dims, jnp.float32)
    if pieces:
        array = array * block_scale(rng, dims, pieces, -0.22, 0.18)
    return jnp.clip(with_spikes(array, jax.random.fold_in(rng, 3), *heavy), -limit, limit).astype(kind)


def setup_inputs(seed: int = 0) -> dict:
    key_of = jax.random.split(jax.random.key(seed), 3)
    return {
        "activations": bell_draw_with(key_of[0], (TOKENS, D), 1.0, 24.0, ((0, 512),), (0, 1, 512, 6.0)),
        "out_grads": bell_draw(key_of[1], (TOKENS, COLS), 1.0, 6.0, ((0, 512),)),
    }


EPSILON = 1e-06

def hadamard(length):
    positions = jnp.arange(length, dtype=jnp.int32)
    shared_bits = positions[:, None] & positions[None, :]
    parity = jnp.zeros((length, length), jnp.int32)
    for shift_bit in range(length.bit_length() - 1):
        parity = parity + (shared_bits >> shift_bit & 1)
    return (1 - 2 * (parity % 2)).astype(jnp.float32) / math.sqrt(length)

def rotate(weight_grad):
    blocked = weight_grad.reshape(-1, BLOCK, weight_grad.shape[-1])
    return jnp.einsum('ij,bjc->bic', hadamard(BLOCK), blocked, precision=lax.Precision.HIGHEST)

def encode(values):
    largest = lax.optimization_barrier(jnp.max(jnp.abs(values), axis=-2))
    scales = jnp.exp2(jnp.ceil(jnp.log2(largest + EPSILON)))
    encoded = (values / scales[..., None, :]).astype(jnp.bfloat16)
    return (encoded, scales.astype(jnp.bfloat16))

def decode(encoded, scales):
    return encoded.astype(jnp.float32) * scales.astype(jnp.float32)[..., None, :]

def reference(activations, out_grads):

    def narrow_group(reduced, wide_index):

        def add_member(partial_value, narrow_index):
            offset = ((narrow_index * N_WIDE + wide_index) * TOK_DEV).astype(jnp.int32)
            act_rows = lax.dynamic_slice_in_dim(activations, offset, TOK_DEV, 0)
            grad_rows = lax.dynamic_slice_in_dim(out_grads, offset, TOK_DEV, 0)
            weight_grad = jnp.dot(act_rows.T, grad_rows, preferred_element_type=jnp.float32)
            encoded, scales = encode(rotate(weight_grad))
            return (partial_value + decode(encoded, scales), None)
        start_partial = jnp.zeros((D // BLOCK, BLOCK, COLS), jnp.float32)
        partial_value, unused = lax.scan(add_member, start_partial, jnp.arange(N_NARROW, dtype=jnp.int32))
        encoded, scales = encode(partial_value)
        return (reduced + decode(encoded, scales), None)
    start_sum = jnp.zeros((D // BLOCK, BLOCK, COLS), jnp.float32)
    reduced, unused = lax.scan(narrow_group, start_sum, jnp.arange(N_WIDE, dtype=jnp.int32))
    return reduced.reshape(D, COLS) / (N_NARROW * N_WIDE)
```

```python
import functools
import math

import jax
import jax.numpy as jnp
from jax import lax
from jax.experimental import pallas as pl
from jax.experimental.pallas import tpu as pltpu
from jax.sharding import PartitionSpec as P

Z, CORES, X, Y = 8, 2, 4, 8
BLOCK = 128
SUB = 16
TOK = 256
WIDTH = X * BLOCK
COLS = 512
F32, BF16 = jnp.float32, jnp.bfloat16
MESH = pl.DeviceIdType.MESH


def kernel(
    act_ref, grad_ref, out_ref,
    a_buf, g_buf, h_buf, m_buf,
    zs, zr, ys, yr, xs, xr,
    z2s, z2r, y2s, y2r, v2s, v2r, w2s, w2r,
    z3s, z3r, y3s, y3r, v3s, v3r, w3s, w3r,
    z_acc, y_acc, v_acc, w_acc,
    load_sem, gload_sem, asend, arecv, gsend, grecv,
    zssem, zrsem, yssem, yrsem, xssem, xrsem, s2sem, r2sem, s3sem, r3sem,
):
    n = lax.axis_index("narrow")
    w = lax.axis_index("wide")
    z, core = n // CORES, n % CORES
    x, y = w // Y, w % Y
    other = 1 - core

    def at_z(d):
        return (((z + d + Z) % Z) * CORES + core, w)

    def at_y(d):
        return (n, x * Y + (y + d + Y) % Y)

    def at_x(d):
        return (n, ((x + d + X) % X) * Y + y)

    sibling = (z * CORES + other, w)

    def own_load(k):
        return pltpu.make_async_copy(
            act_ref.at[:, pl.ds(k * (CORES * WIDTH) + core * WIDTH, WIDTH)],
            a_buf.at[k, pl.ds(core * TOK, TOK), :],
            load_sem.at[k],
        )

    def swap(k):
        return pltpu.make_async_remote_copy(
            src_ref=act_ref.at[:, pl.ds(k * (CORES * WIDTH) + other * WIDTH, WIDTH)],
            dst_ref=a_buf.at[k, pl.ds(core * TOK, TOK), :],
            send_sem=asend.at[k],
            recv_sem=arecv.at[k],
            device_id=sibling,
            device_id_type=MESH,
        )

    def landed(k):
        return pltpu.make_async_remote_copy(
            src_ref=act_ref.at[:, pl.ds(k * (CORES * WIDTH) + other * WIDTH, WIDTH)],
            dst_ref=a_buf.at[k, pl.ds(other * TOK, TOK), :],
            send_sem=asend.at[k],
            recv_sem=arecv.at[k],
            device_id=sibling,
            device_id_type=MESH,
        )

    def order(i):
        return (z + 4 + i // 2 - (i % 2) * i + 2 * Z) % Z

    g_load = pltpu.make_async_copy(grad_ref, g_buf.at[pl.ds(core * TOK, TOK), :], gload_sem)
    g_swap = pltpu.make_async_remote_copy(
        src_ref=grad_ref,
        dst_ref=g_buf.at[pl.ds(core * TOK, TOK), :],
        send_sem=gsend,
        recv_sem=grecv,
        device_id=sibling,
        device_id_type=MESH,
    )
    g_landed = pltpu.make_async_remote_copy(
        src_ref=grad_ref,
        dst_ref=g_buf.at[pl.ds(other * TOK, TOK), :],
        send_sem=gsend,
        recv_sem=grecv,
        device_id=sibling,
        device_id_type=MESH,
    )
    g_load.start()

    @pl.loop(0, Z)
    def _(i):
        own_load(order(i)).start()

    barrier = pltpu.get_barrier_semaphore()
    pl.semaphore_signal(barrier, inc=1, device_id=sibling, device_id_type=MESH)
    for d in range(1, Z):
        pl.semaphore_signal(barrier, inc=1, device_id=at_z(d), device_id_type=MESH)
    for d in range(1, Y):
        pl.semaphore_signal(barrier, inc=1, device_id=at_y(d), device_id_type=MESH)
    for d in range(1, X):
        pl.semaphore_signal(barrier, inc=1, device_id=at_x(d), device_id_type=MESH)

    row = lax.broadcasted_iota(jnp.int32, (BLOCK, BLOCK), 0)
    col = lax.broadcasted_iota(jnp.int32, (BLOCK, BLOCK), 1)
    bits = row & col
    bits = bits ^ (bits >> 4)
    bits = bits ^ (bits >> 2)
    bits = bits ^ (bits >> 1)
    h_buf[...] = (1 - 2 * (bits & 1)).astype(F32).astype(BF16)

    pl.semaphore_wait(barrier, 1 + (Z - 1) + (Y - 1) + (X - 1))

    g_swap.start()

    @pl.loop(0, Z)
    def _(i):
        swap(order(i)).start()

    g_load.wait()
    g_landed.wait_recv()

    def compute(i):
        k = order(i)
        own_load(k).wait()
        landed(k).wait_recv()
        for b in range(X):
            turned = lax.dot_general(
                h_buf[...],
                a_buf[k, :, b * BLOCK : (b + 1) * BLOCK],
                (((1,), (1,)), ((), ())),
                preferred_element_type=F32,
            ).astype(BF16)
            m_buf[k, b] = jnp.dot(turned, g_buf[...], preferred_element_type=F32)

    def send(src, dst, ssem, rsem, target):
        copy = pltpu.make_async_remote_copy(
            src_ref=src, dst_ref=dst, send_sem=ssem, recv_sem=rsem,
            device_id=target, device_id_type=MESH,
        )
        copy.start()
        return copy

    started = []

    def z_own(d, b):
        return m_buf[d, b, :, 0:128]

    def z_step(k):
        for way in range(2):
            sign = 1 - 2 * way
            dest = (z + sign * (Z // 2 - k) + Z) % Z
            low = 2 * way
            if k == 0:
                for b in range(2):
                    zs[way, 0, b] = z_own(dest, low + b).astype(BF16)
                src, dst = zs.at[way, 0, pl.ds(0, 2)], zr.at[way, 0, pl.ds(0, 2)]
            else:
                started[zi[way, k - 1]].wait_recv()
                for b in range(X):
                    if k == 1:
                        if low <= b < low + 2:
                            zs[way, k, b] = (z_own(dest, b) + zr[way, 0, b - low].astype(F32)).astype(BF16)
                        else:
                            zs[way, k, b] = z_own(dest, b).astype(BF16)
                    else:
                        zs[way, k, b] = (z_own(dest, b) + zr[way, k - 1, b].astype(F32)).astype(BF16)
                src, dst = zs.at[way, k], zr.at[way, k]
            zi[way, k] = len(started)
            started.append(send(src, dst, zssem.at[way, k], zrsem.at[way, k], at_z(sign)))

    def y_own(d, k):
        return m_buf[k, :, pl.ds(pl.multiple_of(d * SUB, SUB), SUB), 128:256]

    def y_step(k):
        for way in range(2):
            sign = 1 - 2 * way
            dest = (y + sign * (Y // 2 - k) + Y) % Y
            low = 4 * way
            if k == 0:
                for p in range(4):
                    ys[way, 0, p] = y_own(dest, low + p).astype(BF16)
                src, dst = ys.at[way, 0, pl.ds(0, 4)], yr.at[way, 0, pl.ds(0, 4)]
            else:
                started[yi[way, k - 1]].wait_recv()
                for p in range(Z):
                    if k == 1:
                        if low <= p < low + 4:
                            ys[way, k, p] = (y_own(dest, p) + yr[way, 0, p - low].astype(F32)).astype(BF16)
                        else:
                            ys[way, k, p] = y_own(dest, p).astype(BF16)
                    else:
                        ys[way, k, p] = (y_own(dest, p) + yr[way, k - 1, p].astype(F32)).astype(BF16)
                src, dst = ys.at[way, k], yr.at[way, k]
            yi[way, k] = len(started)
            started.append(send(src, dst, yssem.at[way, k], yrsem.at[way, k], at_y(sign)))

    def x_own(d, k):
        return m_buf[k, d, :, 256:512]

    def x_step(k):
        for way in range(2):
            sign = 1 - 2 * way
            dest = (x + sign * (X // 2 - k) + X) % X
            low = 4 * way
            if k == 0:
                @pl.loop(0, 4)
                def _(p):
                    xs[way, 0, p] = x_own(dest, low + p).astype(BF16)
                src, dst = xs.at[way, 0, pl.ds(0, 4)], xr.at[way, 0, pl.ds(0, 4)]
            else:
                started[xi[way, k - 1]].wait_recv()

                @pl.loop(0, 4)
                def _(p):
                    xs[way, 1, low + p] = (x_own(dest, low + p) + xr[way, 0, p].astype(F32)).astype(BF16)
                    xs[way, 1, 4 - low + p] = x_own(dest, 4 - low + p).astype(BF16)
                src, dst = xs.at[way, k], xr.at[way, k]
            xi[way, k] = len(started)
            started.append(send(src, dst, xssem.at[way, k], xrsem.at[way, k], at_x(sign)))

    zi, yi, xi = {}, {}, {}

    compute(0)
    z_step(0)

    @pl.loop(1, Z)
    def _(i):
        compute(i)

    x_step(0)
    y_step(0)
    z_step(1)
    y_step(1)
    z_step(2)
    y_step(2)
    x_step(1)
    z_step(3)
    y_step(3)

    def drain(buf, sem):
        pltpu.make_async_copy(buf, buf, sem).wait()

    def rows_of(d):
        return pl.ds(pl.multiple_of(d * SUB, SUB), SUB)

    for way in range(2):
        started[zi[way, 3]].wait_recv()
    for j in range(1, Y + 1):
        d = (y + j) % Y
        part = (
            m_buf[z, :, rows_of(d), 0:128]
            + zr[0, 3, :, rows_of(d), :].astype(F32)
            + zr[1, 3, :, rows_of(d), :].astype(F32)
        )
        if j < Y:
            z2s[j - 1] = part.astype(BF16)
            send(z2s.at[j - 1], z2r.at[j - 1], s2sem.at[0], r2sem.at[0], at_y(j))
        else:
            z_acc[...] = part

    for way in range(2):
        started[yi[way, 3]].wait_recv()
    for j in range(1, Z + 1):
        d = (z + j) % Z
        part = (
            m_buf[d, :, rows_of(y), 128:256]
            + yr[0, 3, d].astype(F32)
            + yr[1, 3, d].astype(F32)
        )
        if j < Z:
            y2s[j - 1] = part.astype(BF16)
            send(y2s.at[j - 1], y2r.at[j - 1], s2sem.at[1], r2sem.at[1], at_z(j))
        else:
            y_acc[...] = part

    def x_third(s2, r2, acc, s3, r3, at):
        drain(r2, r2sem.at[at])
        for j in range(1, X + 1):
            d = (x + j) % X
            part = acc[d]
            for q in range(r2.shape[0]):
                part = part + r2[q, d].astype(F32)
            if j < X:
                s3[j - 1] = part.astype(BF16)
                send(s3.at[j - 1], r3.at[j - 1], s3sem.at[at], r3sem.at[at], at_x(j))
            else:
                acc[0] = part

    x_third(z2s, z2r, z_acc, z3s, z3r, 0)
    x_third(y2s, y2r, y_acc, y3s, y3r, 1)

    for way in range(2):
        started[xi[way, 1]].wait_recv()
    for j in range(1, Y + 1):
        d = (y + j) % Y
        part = (
            m_buf[:, x, rows_of(d), 256:384]
            + xr[0, 1, :, rows_of(d), 0:128].astype(F32)
            + xr[1, 1, :, rows_of(d), 0:128].astype(F32)
        )
        if j < Y:
            v2s[j - 1] = part.astype(BF16)
            send(v2s.at[j - 1], v2r.at[j - 1], s2sem.at[2], r2sem.at[2], at_y(j))
        else:
            v_acc[...] = part
        d = (z + j) % Z
        part = (
            m_buf[d, x, :, 384:512]
            + xr[0, 1, d, :, 128:256].astype(F32)
            + xr[1, 1, d, :, 128:256].astype(F32)
        )
        if j < Z:
            w2s[j - 1] = part.astype(BF16)
            send(w2s.at[j - 1], w2r.at[j - 1], s2sem.at[3], r2sem.at[3], at_z(j))
        else:
            w_acc[...] = part

    scale = 1.0 / (Z * CORES * X * Y * math.sqrt(BLOCK))

    def finish(own, r3, at, first):
        drain(r3, r3sem.at[at])
        total = own
        for q in range(r3.shape[0]):
            total = total + r3[q].astype(F32)
        out_ref[:, first : first + 128] = total * scale

    finish(z_acc[0], z3r, 0, 0)
    finish(y_acc[0], y3r, 1, 128)

    drain(v2r, r2sem.at[2])
    for j in range(1, Z + 1):
        d = (z + j) % Z
        part = v_acc[d]
        for q in range(Y - 1):
            part = part + v2r[q, d].astype(F32)
        if j < Z:
            v3s[j - 1] = part.astype(BF16)
            send(v3s.at[j - 1], v3r.at[j - 1], s3sem.at[2], r3sem.at[2], at_z(j))
        else:
            v_own = part
    drain(w2r, r2sem.at[3])
    for j in range(1, Y + 1):
        d = (y + j) % Y
        part = w_acc[rows_of(d), :]
        for q in range(Z - 1):
            part = part + w2r[q, rows_of(d), :].astype(F32)
        if j < Y:
            w3s[j - 1] = part.astype(BF16)
            send(w3s.at[j - 1], w3r.at[j - 1], s3sem.at[3], r3sem.at[3], at_y(j))
        else:
            w_own = part
    finish(v_own, v3r, 2, 256)
    finish(w_own, w3r, 3, 384)

    g_swap.wait_send()

    @pl.loop(0, Z)
    def _(k):
        swap(k).wait_send()

    for copy in started:
        copy.wait_send()
    for at, buf in enumerate((z2s, y2s, v2s, w2s)):
        drain(buf, s2sem.at[at])
    for at, buf in enumerate((z3s, y3s, v3s, w3s)):
        drain(buf, s3sem.at[at])


def per_device(activations, out_grads):
    def vm(*shape, dtype=BF16):
        return pltpu.VMEM(shape, dtype)

    dma = pltpu.SemaphoreType.DMA
    scratch = [
        vm(Z, CORES * TOK, WIDTH), vm(CORES * TOK, COLS), vm(BLOCK, BLOCK),
        vm(Z, X, BLOCK, COLS, dtype=F32),
        vm(2, 4, X, BLOCK, 128), vm(2, 4, X, BLOCK, 128),
        vm(2, 4, Z, X, SUB, 128), vm(2, 4, Z, X, SUB, 128),
        vm(2, 2, Z, BLOCK, 256), vm(2, 2, Z, BLOCK, 256),
        vm(Y - 1, X, SUB, 128), vm(Y - 1, X, SUB, 128),
        vm(Z - 1, X, SUB, 128), vm(Z - 1, X, SUB, 128),
        vm(Y - 1, Z, SUB, 128), vm(Y - 1, Z, SUB, 128),
        vm(Z - 1, BLOCK, 128), vm(Z - 1, BLOCK, 128),
        vm(X - 1, SUB, 128), vm(X - 1, SUB, 128),
        vm(X - 1, SUB, 128), vm(X - 1, SUB, 128),
        vm(Z - 1, SUB, 128), vm(Z - 1, SUB, 128),
        vm(Y - 1, SUB, 128), vm(Y - 1, SUB, 128),
        vm(X, SUB, 128, dtype=F32), vm(X, SUB, 128, dtype=F32),
        vm(Z, SUB, 128, dtype=F32), vm(BLOCK, 128, dtype=F32),
        dma((Z,)), dma, dma((Z,)), dma((Z,)), dma, dma,
        dma((2, 4)), dma((2, 4)), dma((2, 4)), dma((2, 4)), dma((2, 2)), dma((2, 2)),
        dma((4,)), dma((4,)), dma((4,)), dma((4,)),
    ]
    return pl.pallas_call(
        kernel,
        out_shape=jax.ShapeDtypeStruct((SUB, COLS), F32),
        in_specs=[pl.BlockSpec(memory_space=pl.ANY)] * 2,
        out_specs=pl.BlockSpec(memory_space=pltpu.VMEM),
        scratch_shapes=scratch,
        compiler_params=pltpu.CompilerParams(
            collective_id=0, has_side_effects=True, vmem_limit_bytes=48 * 1024 * 1024
        ),
        cost_estimate=pl.CostEstimate(
            flops=2 * CORES * TOK * Z * WIDTH * (COLS + BLOCK),
            bytes_accessed=TOK * (2 * Z * WIDTH + COLS) * 2,
            transcendentals=0,
        ),
    )(activations, out_grads)


def solution(mesh):
    return jax.shard_map(
        per_device,
        mesh=mesh,
        in_specs=(P(("narrow", "wide"), None), P(("narrow", "wide"), None)),
        out_specs=P(("narrow", "wide"), None),
        check_vma=False,
    )
```

```python
import math

import jax
import jax.numpy as jnp
from jax import lax
from jax.experimental import pallas as pl
from jax.experimental.pallas import tpu as pltpu
from jax.sharding import PartitionSpec as P

Z, CORES, X, Y = 8, 2, 4, 8
BLOCK = 128
HALF = BLOCK // 2
SUB = 16
TOK = 256
WIDTH = X * BLOCK
COLS = 512
F32, BF16 = jnp.float32, jnp.bfloat16
MESH = pl.DeviceIdType.MESH

OFFSET = (4, 3, 5, 2, 6, 1, 7, 0)
STEP = {offset: i for i, offset in enumerate(OFFSET)}


def kernel(
    act_ref, grad_ref, out_ref,
    a_buf, g_buf, h_buf, m_buf,
    zs, zr, ys, yr, xs0, xr0, xs1, xr1, vs, vr,
    z2s, z2r, y2s, y2r, v2s, v2r, z3s, z3r, y3s, y3r,
    z_acc, y_acc,
    load_sem, gload_sem, asend, arecv, gsend, grecv,
    zssem, zrsem, yssem, yrsem, x0ssem, x0rsem, x1ssem, x1rsem, vssem, vrsem,
    s2sem, r2sem, s3sem, r3sem,
):
    n = lax.axis_index("narrow")
    w = lax.axis_index("wide")
    z, core = n // CORES, n % CORES
    x, y = w // Y, w % Y
    other = 1 - core

    def at_z(d):
        return (((z + d + Z) % Z) * CORES + core, w)

    def at_y(d):
        return (n, x * Y + (y + d + Y) % Y)

    def at_x(d):
        return (n, ((x + d + X) % X) * Y + y)

    sibling = (z * CORES + other, w)

    def remote(src, dst, ssem, rsem, target):
        return pltpu.make_async_remote_copy(
            src_ref=src, dst_ref=dst, send_sem=ssem, recv_sem=rsem,
            device_id=target, device_id_type=MESH,
        )

    def place(i):
        return (z + 4 + i // 2 - (i % 2) * i + 2 * Z) % Z

    def own_load(i):
        return pltpu.make_async_copy(
            act_ref.at[:, pl.ds((place(i) * CORES + core) * WIDTH, WIDTH)],
            a_buf.at[i, pl.ds(core * TOK, TOK), :],
            load_sem.at[i],
        )

    def swap(i, half):
        return remote(
            act_ref.at[:, pl.ds((place(i) * CORES + other) * WIDTH, WIDTH)],
            a_buf.at[i, pl.ds(half * TOK, TOK), :],
            asend.at[i], arecv.at[i], sibling,
        )

    def g_swap(half):
        return remote(grad_ref, g_buf.at[pl.ds(half * TOK, TOK), :], gsend, grecv, sibling)

    g_load = pltpu.make_async_copy(grad_ref, g_buf.at[pl.ds(core * TOK, TOK), :], gload_sem)

    barrier = pltpu.get_barrier_semaphore()
    pl.semaphore_signal(barrier, inc=1, device_id=sibling, device_id_type=MESH)
    for d in range(1, Z):
        pl.semaphore_signal(barrier, inc=1, device_id=at_z(d), device_id_type=MESH)
    for d in range(1, Y):
        pl.semaphore_signal(barrier, inc=1, device_id=at_y(d), device_id_type=MESH)
    for d in range(1, X):
        pl.semaphore_signal(barrier, inc=1, device_id=at_x(d), device_id_type=MESH)

    g_load.start()

    @pl.loop(0, Z)
    def _(i):
        own_load(i).start()

    row = (lax.broadcasted_iota(jnp.int32, (BLOCK, BLOCK), 0) + y * SUB) & (BLOCK - 1)
    col = lax.broadcasted_iota(jnp.int32, (BLOCK, BLOCK), 1)
    bits = row & col
    bits = bits ^ (bits >> 4)
    bits = bits ^ (bits >> 2)
    bits = bits ^ (bits >> 1)
    h_buf[...] = (1 - 2 * (bits & 1)).astype(F32).astype(BF16)

    pl.semaphore_wait(barrier, 1 + (Z - 1) + (Y - 1) + (X - 1))

    g_swap(core).start()

    @pl.loop(0, Z)
    def _(i):
        swap(i, core).start()

    def compute(i):
        own_load(i).wait()
        swap(i, other).wait_recv()
        for j in range(X):
            b = (x + j) % X
            turned = lax.dot_general(
                h_buf[...],
                a_buf[i, :, pl.ds(pl.multiple_of(b * BLOCK, BLOCK), BLOCK)],
                (((1,), (1,)), ((), ())),
                preferred_element_type=F32,
            ).astype(BF16)
            m_buf[i, j] = jnp.dot(turned, g_buf[...], preferred_element_type=F32)

    def way_sign(way):
        return 1 - 2 * way

    def z_copy(way, h, k):
        return remote(
            zs.at[way, h, k], zr.at[way, h, k], zssem.at[way, h, k], zrsem.at[way, h, k],
            at_z(way_sign(way)),
        )

    def z_step(way, h, k):
        i = STEP[(way_sign(way) * (4 - k)) % Z]
        if k >= 2 or (k == 1 and h == way):
            z_copy(way, h, k - 1).wait_recv()
            for j in range(2):
                zs[way, h, k, j] = (
                    m_buf[i, 2 * h + j, :, 0:128] + zr[way, h, k - 1, j].astype(F32)
                ).astype(BF16)
        else:
            for j in range(2):
                zs[way, h, k, j] = m_buf[i, 2 * h + j, :, 0:128].astype(BF16)
        z_copy(way, h, k).start()

    def y_copy(way, g, k):
        return remote(
            ys.at[way, g, k], yr.at[way, g, k], yssem.at[way, g, k], yrsem.at[way, g, k],
            at_y(way_sign(way)),
        )

    def y_step(way, g, k):
        first = ((way_sign(way) * (4 - k)) % Y) * SUB
        if k >= 2 or (k == 1 and g == way):
            y_copy(way, g, k - 1).wait_recv()
            for p in range(4):
                ys[way, g, k, p] = (
                    m_buf[4 * g + p, :, first : first + SUB, 128:256]
                    + yr[way, g, k - 1, p].astype(F32)
                ).astype(BF16)
        else:
            for p in range(4):
                ys[way, g, k, p] = m_buf[4 * g + p, :, first : first + SUB, 128:256].astype(BF16)
        y_copy(way, g, k).start()

    def x0_copy(way, i):
        return remote(
            xs0.at[i, way], xr0.at[i, way], x0ssem.at[i, way], x0rsem.at[i, way],
            at_x(way_sign(way)),
        )

    def x1_copy(way, i):
        return remote(
            xs1.at[i, way], xr1.at[i, way], x1ssem.at[i, way], x1rsem.at[i, way],
            at_x(way_sign(way)),
        )

    def v_copy(way, k):
        if k == 0:
            src, dst = vs.at[way, 0, pl.ds(0, HALF)], vr.at[way, 0, pl.ds(0, HALF)]
        else:
            src, dst = vs.at[way, k], vr.at[way, k]
        return remote(src, dst, vssem.at[way, k], vrsem.at[way, k], at_z(way_sign(way)))

    def x0_step(i):
        for way in range(2):
            xs0[i, way] = m_buf[i, 2, way * HALF : (way + 1) * HALF, 256:512].astype(BF16)
            x0_copy(way, i).start()

    def x1_step(i):
        for way in range(2):
            j = 1 + 2 * way
            x0_copy(way, i).wait_recv()
            mine = slice(way * HALF, (way + 1) * HALF)
            rest = slice((1 - way) * HALF, (2 - way) * HALF)
            xs1[i, way, mine] = (m_buf[i, j, mine, 256:512] + xr0[i, way].astype(F32)).astype(BF16)
            xs1[i, way, rest] = m_buf[i, j, rest, 256:512].astype(BF16)
            x1_copy(way, i).start()

    def x2_rows(i, rows):
        return (
            m_buf[i, 0, rows, 256:512]
            + xr1[i, 0, rows].astype(F32)
            + xr1[i, 1, rows].astype(F32)
        )

    def x2_step(i):
        for way in range(2):
            x1_copy(way, i).wait_recv()
        if i == 0:
            for way in range(2):
                vs[way, 0, 0:HALF] = x2_rows(0, slice(way * HALF, (way + 1) * HALF)).astype(BF16)
                v_copy(way, 0).start()
        elif i < Z - 1:
            way, k = 1 - i % 2, (i + 1) // 2
            v_copy(way, k - 1).wait_recv()
            if k == 1:
                mine = slice(way * HALF, (way + 1) * HALF)
                rest = slice((1 - way) * HALF, (2 - way) * HALF)
                vs[way, 1, mine] = (x2_rows(i, mine) + vr[way, 0, 0:HALF].astype(F32)).astype(BF16)
                vs[way, 1, rest] = x2_rows(i, rest).astype(BF16)
            else:
                vs[way, k] = (x2_rows(i, slice(0, BLOCK)) + vr[way, k - 1].astype(F32)).astype(BF16)
            v_copy(way, k).start()
        else:
            for way in range(2):
                v_copy(way, 3).wait_recv()
            own = None
            for j in range(Y):
                rows = slice(j * SUB, (j + 1) * SUB)
                part = x2_rows(i, rows) + vr[0, 3, rows].astype(F32) + vr[1, 3, rows].astype(F32)
                if j == 0:
                    own = part
                else:
                    v2s[j - 1] = part.astype(BF16)
                    remote(v2s.at[j - 1], v2r.at[j - 1], s2sem.at[2], r2sem.at[2], at_y(j)).start()
            return own

    def drain(buf, sem):
        pltpu.make_async_copy(buf, buf, sem).wait()

    def z_second():
        for way in range(2):
            for h in range(2):
                z_copy(way, h, 3).wait_recv()
        for j in range(Y):
            rows = slice(j * SUB, (j + 1) * SUB)
            for h in range(2):
                part = (
                    m_buf[Z - 1, 2 * h : 2 * h + 2, rows, 0:128]
                    + zr[0, h, 3, :, rows].astype(F32)
                    + zr[1, h, 3, :, rows].astype(F32)
                )
                if j == 0:
                    z_acc[2 * h : 2 * h + 2] = part
                else:
                    z2s[j - 1, 2 * h : 2 * h + 2] = part.astype(BF16)
            if j > 0:
                remote(z2s.at[j - 1], z2r.at[j - 1], s2sem.at[0], r2sem.at[0], at_y(j)).start()

    def y_second():
        for way in range(2):
            for g in range(2):
                y_copy(way, g, 3).wait_recv()
        for j in range(Z):
            i = STEP[j]
            part = (
                m_buf[i, :, 0:SUB, 128:256]
                + yr[0, i // 4, 3, i % 4].astype(F32)
                + yr[1, i // 4, 3, i % 4].astype(F32)
            )
            if j == 0:
                y_acc[...] = part
            else:
                y2s[j - 1] = part.astype(BF16)
                remote(y2s.at[j - 1], y2r.at[j - 1], s2sem.at[1], r2sem.at[1], at_z(j)).start()

    def third(r2, acc, s3, r3, at):
        drain(r2, r2sem.at[at])
        own = None
        for j in range(X):
            part = acc[j]
            for q in range(r2.shape[0]):
                part = part + r2[q, j].astype(F32)
            if j == 0:
                own = part
            else:
                s3[j - 1] = part.astype(BF16)
                remote(s3.at[j - 1], r3.at[j - 1], s3sem.at[at], r3sem.at[at], at_x(j)).start()
        return own

    scale = 1.0 / (Z * CORES * X * Y * math.sqrt(BLOCK))

    def finish(own, received, sem, first, last):
        drain(received, sem)
        total = own
        for q in range(received.shape[0]):
            total = total + received[q].astype(F32)
        out_ref[:, first:last] = total * scale

    g_load.wait()
    g_swap(other).wait_recv()

    @pl.loop(0, Z)
    def _(i):
        compute(i)
        x0_step(i)

        @pl.when(i == 0)
        def _():
            z_step(0, 0, 0)
            z_step(1, 1, 0)

        @pl.when(i == 2)
        def _():
            z_step(0, 1, 1)
            z_step(1, 0, 1)

        @pl.when(i == 3)
        def _():
            y_step(0, 0, 0)
            y_step(1, 0, 1)

    y_step(1, 1, 0)
    y_step(0, 1, 1)
    z_step(0, 0, 1)
    z_step(1, 1, 1)
    x1_step(0)
    y_step(0, 0, 1)
    y_step(1, 0, 2)
    x1_step(1)
    z_step(0, 1, 2)
    z_step(1, 0, 2)
    x1_step(2)
    y_step(1, 1, 1)
    y_step(0, 1, 2)
    x2_step(0)
    x1_step(3)
    z_step(0, 0, 2)
    z_step(1, 1, 2)
    x2_step(1)
    y_step(0, 0, 2)
    y_step(1, 0, 3)
    x1_step(4)
    z_step(0, 1, 3)
    z_step(1, 0, 3)
    x2_step(2)
    x1_step(5)
    y_step(1, 1, 2)
    y_step(0, 1, 3)
    z_step(0, 0, 3)
    z_step(1, 1, 3)
    x2_step(3)
    x1_step(6)
    y_step(0, 0, 3)
    y_step(1, 1, 3)
    x1_step(7)
    x2_step(4)
    z_second()
    x2_step(5)
    y_second()
    x2_step(6)
    z_own = third(z2r, z_acc, z3s, z3r, 0)
    y_own = third(y2r, y_acc, y3s, y3r, 1)
    v_own = x2_step(7)
    finish(z_own, z3r, r3sem.at[0], 0, 128)
    finish(y_own, y3r, r3sem.at[1], 128, 256)
    finish(v_own, v2r, r2sem.at[2], 256, 512)

    g_swap(core).wait_send()

    @pl.loop(0, Z)
    def _(i):
        swap(i, core).wait_send()
        for way in range(2):
            x0_copy(way, i).wait_send()
            x1_copy(way, i).wait_send()

    for way in range(2):
        for k in range(4):
            v_copy(way, k).wait_send()
            for part in range(2):
                if k > 0 or part == way:
                    z_copy(way, part, k).wait_send()
                    y_copy(way, part, k).wait_send()
    for at, buf in enumerate((z2s, y2s, v2s)):
        drain(buf, s2sem.at[at])
    for at, buf in enumerate((z3s, y3s)):
        drain(buf, s3sem.at[at])


def per_device(activations, out_grads):
    def vm(*shape, dtype=BF16):
        return pltpu.VMEM(shape, dtype)

    dma = pltpu.SemaphoreType.DMA
    scratch = [
        vm(Z, CORES * TOK, WIDTH), vm(CORES * TOK, COLS), vm(BLOCK, BLOCK),
        vm(Z, X, BLOCK, COLS, dtype=F32),
        vm(2, 2, 4, 2, BLOCK, 128), vm(2, 2, 4, 2, BLOCK, 128),
        vm(2, 2, 4, 4, X, SUB, 128), vm(2, 2, 4, 4, X, SUB, 128),
        vm(Z, 2, HALF, 256), vm(Z, 2, HALF, 256),
        vm(Z, 2, BLOCK, 256), vm(Z, 2, BLOCK, 256),
        vm(2, 4, BLOCK, 256), vm(2, 4, BLOCK, 256),
        vm(Y - 1, X, SUB, 128), vm(Y - 1, X, SUB, 128),
        vm(Z - 1, X, SUB, 128), vm(Z - 1, X, SUB, 128),
        vm(Y - 1, SUB, 256), vm(Y - 1, SUB, 256),
        vm(X - 1, SUB, 128), vm(X - 1, SUB, 128),
        vm(X - 1, SUB, 128), vm(X - 1, SUB, 128),
        vm(X, SUB, 128, dtype=F32), vm(X, SUB, 128, dtype=F32),
        dma((Z,)), dma, dma((Z,)), dma((Z,)), dma, dma,
        dma((2, 2, 4)), dma((2, 2, 4)), dma((2, 2, 4)), dma((2, 2, 4)),
        dma((Z, 2)), dma((Z, 2)), dma((Z, 2)), dma((Z, 2)), dma((2, 4)), dma((2, 4)),
        dma((3,)), dma((3,)), dma((2,)), dma((2,)),
    ]
    return pl.pallas_call(
        kernel,
        out_shape=jax.ShapeDtypeStruct((SUB, COLS), F32),
        in_specs=[pl.BlockSpec(memory_space=pl.ANY)] * 2,
        out_specs=pl.BlockSpec(memory_space=pltpu.VMEM),
        scratch_shapes=scratch,
        compiler_params=pltpu.CompilerParams(
            collective_id=0, has_side_effects=True, vmem_limit_bytes=60 * 1024 * 1024
        ),
        cost_estimate=pl.CostEstimate(
            flops=2 * CORES * TOK * Z * WIDTH * (COLS + BLOCK),
            bytes_accessed=TOK * (2 * Z * WIDTH + COLS) * 2,
            transcendentals=0,
        ),
    )(activations, out_grads)


def solution(mesh):
    return jax.shard_map(
        per_device,
        mesh=mesh,
        in_specs=(P(("narrow", "wide"), None), P(("narrow", "wide"), None)),
        out_specs=P(("narrow", "wide"), None),
        check_vma=False,
    )
```

```python
import math

import jax
import jax.numpy as jnp
from jax import lax
from jax.experimental import pallas as pl
from jax.experimental.pallas import tpu as pltpu
from jax.sharding import PartitionSpec as P

Z, CORES, X, Y = 8, 2, 4, 8
BLOCK = 128
HALF = BLOCK // 2
SUB = 16
TOK = 256
WIDTH = X * BLOCK
COLS = 512
F32, BF16 = jnp.float32, jnp.bfloat16
MESH = pl.DeviceIdType.MESH

OFFSET = (4, 3, 5, 2, 6, 1, 7, 0)
STEP = {offset: i for i, offset in enumerate(OFFSET)}
AHEAD = 3


def kernel(
    act_ref, grad_ref, out_ref,
    a_buf, g_buf, h_buf, t_buf, m_buf,
    zs, zr, ys, yr, xs0, xr0, xs1, xr1, vs, vr,
    z2s, z2r, y2s, y2r, v2s, v2r, z3s, z3r, y3s, y3r,
    z_acc, y_acc, v_acc,
    load_sem, gload_sem, asend, arecv, gsend, grecv,
    zssem, zrsem, yssem, yrsem, x0ssem, x0rsem, x1ssem, x1rsem, vssem, vrsem,
    s2sem, r2sem, s3sem, r3sem,
):
    n = lax.axis_index("narrow")
    w = lax.axis_index("wide")
    z, core = n // CORES, n % CORES
    x, y = w // Y, w % Y
    other = 1 - core

    def at_z(d):
        return (((z + d + Z) % Z) * CORES + core, w)

    def at_y(d):
        return (n, x * Y + (y + d + Y) % Y)

    def at_x(d):
        return (n, ((x + d + X) % X) * Y + y)

    sibling = (z * CORES + other, w)

    def remote(src, dst, ssem, rsem, target):
        return pltpu.make_async_remote_copy(
            src_ref=src, dst_ref=dst, send_sem=ssem, recv_sem=rsem,
            device_id=target, device_id_type=MESH,
        )

    def place(i):
        return (z + 4 + i // 2 - (i % 2) * i + 2 * Z) % Z

    def own_load(i):
        return pltpu.make_async_copy(
            act_ref.at[:, pl.ds((place(i) * CORES + core) * WIDTH, WIDTH)],
            a_buf.at[i, pl.ds(core * TOK, TOK), :],
            load_sem.at[i],
        )

    def swap(i, half):
        return remote(
            act_ref.at[:, pl.ds((place(i) * CORES + other) * WIDTH, WIDTH)],
            a_buf.at[i, pl.ds(half * TOK, TOK), :],
            asend.at[i], arecv.at[i], sibling,
        )

    def g_swap(half):
        return remote(grad_ref, g_buf.at[pl.ds(half * TOK, TOK), :], gsend, grecv, sibling)

    g_load = pltpu.make_async_copy(grad_ref, g_buf.at[pl.ds(core * TOK, TOK), :], gload_sem)

    barrier = pltpu.get_barrier_semaphore()
    pl.semaphore_signal(barrier, inc=1, device_id=sibling, device_id_type=MESH)
    for d in range(1, Z):
        pl.semaphore_signal(barrier, inc=1, device_id=at_z(d), device_id_type=MESH)
    for d in range(1, Y):
        pl.semaphore_signal(barrier, inc=1, device_id=at_y(d), device_id_type=MESH)
    for d in range(1, X):
        pl.semaphore_signal(barrier, inc=1, device_id=at_x(d), device_id_type=MESH)

    g_load.start()

    @pl.loop(0, Z)
    def _(i):
        own_load(i).start()

    row = (lax.broadcasted_iota(jnp.int32, (BLOCK, BLOCK), 0) + y * SUB) & (BLOCK - 1)
    col = lax.broadcasted_iota(jnp.int32, (BLOCK, BLOCK), 1)
    bits = row & col
    bits = bits ^ (bits >> 4)
    bits = bits ^ (bits >> 2)
    bits = bits ^ (bits >> 1)
    h_buf[...] = (1 - 2 * (bits & 1)).astype(F32).astype(BF16)

    pl.semaphore_wait(barrier, 1 + (Z - 1) + (Y - 1) + (X - 1))

    g_swap(core).start()

    for i in range(AHEAD):
        swap(i, core).start()

    def compute(i):
        own_load(i).wait()
        swap(i, other).wait_recv()
        if i + AHEAD < Z:
            swap(i + AHEAD, core).start()
        for j in range(X):
            b = (x + j) % X
            t_buf[j * BLOCK : (j + 1) * BLOCK] = lax.dot_general(
                h_buf[...],
                a_buf[i, :, pl.ds(pl.multiple_of(b * BLOCK, BLOCK), BLOCK)],
                (((1,), (1,)), ((), ())),
                preferred_element_type=F32,
            ).astype(BF16)
        m_buf[i] = jnp.dot(t_buf[...], g_buf[...], preferred_element_type=F32).reshape(X, BLOCK, COLS)

    def way_sign(way):
        return 1 - 2 * way

    def z_copy(way, j, k):
        return remote(
            zs.at[way, j, k], zr.at[way, j, k], zssem.at[way, j, k], zrsem.at[way, j, k],
            at_z(way_sign(way)),
        )

    def begins(way, j):
        return j // 2 == way

    def z_step(way, j, k):
        i = STEP[(way_sign(way) * (4 - k)) % Z]
        part = m_buf[i, j, :, 0:128]
        if k >= 2 or (k == 1 and begins(way, j)):
            z_copy(way, j, k - 1).wait_recv()
            part = part + zr[way, j, k - 1].astype(F32)
        zs[way, j, k] = part.astype(BF16)
        z_copy(way, j, k).start()

    def y_copy(way, j, k):
        return remote(
            ys.at[way, j, k], yr.at[way, j, k], yssem.at[way, j, k], yrsem.at[way, j, k],
            at_y(way_sign(way)),
        )

    def y_step(way, j, k):
        first = ((way_sign(way) * (4 - k)) % Y) * SUB
        part = m_buf[:, j, first : first + SUB, 128:256]
        if k >= 2 or (k == 1 and begins(way, j)):
            y_copy(way, j, k - 1).wait_recv()
            part = part + yr[way, j, k - 1].astype(F32)
        ys[way, j, k] = part.astype(BF16)
        y_copy(way, j, k).start()

    def x0_copy(way, i):
        return remote(
            xs0.at[i, way], xr0.at[i, way], x0ssem.at[i, way], x0rsem.at[i, way],
            at_x(way_sign(way)),
        )

    def x1_copy(way, i):
        return remote(
            xs1.at[i, way], xr1.at[i, way], x1ssem.at[i, way], x1rsem.at[i, way],
            at_x(way_sign(way)),
        )

    def v_copy(way, k, h):
        if k == 0:
            src, dst = vs.at[way, 0, h, pl.ds(0, HALF)], vr.at[way, 0, h, pl.ds(0, HALF)]
        else:
            src, dst = vs.at[way, k, h], vr.at[way, k, h]
        return remote(src, dst, vssem.at[way, k, h], vrsem.at[way, k, h], at_z(way_sign(way)))

    def w_copy(j, h):
        return remote(
            v2s.at[h, j - 1], v2r.at[h, j - 1], s2sem.at[2 + h], r2sem.at[2 + h], at_y(j)
        )

    def x0_step(i):
        for way in range(2):
            xs0[i, way] = m_buf[i, 2, way * HALF : (way + 1) * HALF, 256:512].astype(BF16)
            x0_copy(way, i).start()

    def x1_step(i):
        for way in range(2):
            j = 1 + 2 * way
            x0_copy(way, i).wait_recv()
            mine = slice(way * HALF, (way + 1) * HALF)
            rest = slice((1 - way) * HALF, (2 - way) * HALF)
            xs1[i, way, mine] = (m_buf[i, j, mine, 256:512] + xr0[i, way].astype(F32)).astype(BF16)
            xs1[i, way, rest] = m_buf[i, j, rest, 256:512].astype(BF16)
            x1_copy(way, i).start()

    def x2_rows(i, rows, h):
        there = slice(h * 128, (h + 1) * 128)
        return (
            m_buf[i, 0, rows, 256 + h * 128 : 384 + h * 128]
            + xr1[i, 0, rows, there].astype(F32)
            + xr1[i, 1, rows, there].astype(F32)
        )

    def v_step(i, h):
        if i == 0:
            for way in range(2):
                rows = slice(way * HALF, (way + 1) * HALF)
                vs[way, 0, h, 0:HALF] = x2_rows(0, rows, h).astype(BF16)
                v_copy(way, 0, h).start()
            return
        if i < Z - 1:
            way, k = 1 - i % 2, (i + 1) // 2
            v_copy(way, k - 1, h).wait_recv()
            if k == 1:
                mine = slice(way * HALF, (way + 1) * HALF)
                rest = slice((1 - way) * HALF, (2 - way) * HALF)
                vs[way, 1, h, mine] = (
                    x2_rows(i, mine, h) + vr[way, 0, h, 0:HALF].astype(F32)
                ).astype(BF16)
                vs[way, 1, h, rest] = x2_rows(i, rest, h).astype(BF16)
            else:
                vs[way, k, h] = (
                    x2_rows(i, slice(0, BLOCK), h) + vr[way, k - 1, h].astype(F32)
                ).astype(BF16)
            v_copy(way, k, h).start()
            return
        for way in range(2):
            v_copy(way, 3, h).wait_recv()
        part = (
            x2_rows(i, slice(0, BLOCK), h) + vr[0, 3, h].astype(F32) + vr[1, 3, h].astype(F32)
        )
        v_acc[h] = part[0:SUB]
        for j in range(1, Y):
            v2s[h, j - 1] = part[j * SUB : (j + 1) * SUB].astype(BF16)
            w_copy(j, h).start()

    def x1_arrived(i):
        for way in range(2):
            x1_copy(way, i).wait_recv()

    def drain(buf, sem):
        pltpu.make_async_copy(buf, buf, sem).wait()

    def z2_step(j):
        for way in range(2):
            z_copy(way, j, 3).wait_recv()
        part = m_buf[Z - 1, j, :, 0:128] + zr[0, j, 3].astype(F32) + zr[1, j, 3].astype(F32)
        if j == 0:
            z_acc[...] = part
        else:
            z2s[j - 1] = part.astype(BF16)
            remote(z2s.at[j - 1], z2r.at[j - 1], s2sem.at[0], r2sem.at[0], at_x(j)).start()

    def y2_step(j):
        for way in range(2):
            y_copy(way, j, 3).wait_recv()
        part = m_buf[:, j, 0:SUB, 128:256] + yr[0, j, 3].astype(F32) + yr[1, j, 3].astype(F32)
        if j == 0:
            y_acc[...] = part
        else:
            y2s[j - 1] = part.astype(BF16)
            remote(y2s.at[j - 1], y2r.at[j - 1], s2sem.at[1], r2sem.at[1], at_x(j)).start()

    def z3_step():
        drain(z2r, r2sem.at[0])
        part = z_acc[...]
        for q in range(X - 1):
            part = part + z2r[q].astype(F32)
        z_acc[...] = part
        for j in range(1, Y):
            z3s[j - 1] = part[j * SUB : (j + 1) * SUB].astype(BF16)
            remote(z3s.at[j - 1], z3r.at[j - 1], s3sem.at[0], r3sem.at[0], at_y(j)).start()

    def y3_step():
        drain(y2r, r2sem.at[1])
        part = y_acc[...]
        for q in range(X - 1):
            part = part + y2r[q].astype(F32)
        y_acc[...] = part
        for j in range(1, Z):
            y3s[j - 1] = part[STEP[j]].astype(BF16)
            remote(y3s.at[j - 1], y3r.at[j - 1], s3sem.at[1], r3sem.at[1], at_z(j)).start()

    scale = 1.0 / (Z * CORES * X * Y * math.sqrt(BLOCK))

    def finish(own, received, sem, first):
        drain(received, sem)
        total = own
        for q in range(received.shape[0]):
            total = total + received[q].astype(F32)
        out_ref[:, first : first + 128] = total * scale

    g_load.wait()
    g_swap(other).wait_recv()

    compute(0)
    x0_step(0)
    z_step(0, 1, 0)
    compute(1)
    z_step(1, 2, 0)
    z_step(0, 2, 1)
    z_step(1, 3, 0)
    x0_step(1)
    z_step(0, 3, 1)
    z_step(0, 0, 0)
    compute(2)
    compute(3)
    z_step(1, 1, 1)
    x0_step(3)
    z_step(1, 0, 1)
    x0_step(2)
    compute(4)
    x1_step(0)
    compute(5)
    x0_step(4)
    compute(6)
    compute(7)
    y_step(1, 2, 0)
    y_step(0, 2, 1)
    y_step(1, 3, 0)
    x0_step(5)
    z_step(1, 2, 1)
    z_step(1, 3, 1)
    z_step(0, 1, 1)
    y_step(1, 0, 1)
    y_step(1, 1, 1)
    x0_step(6)
    x1_step(2)
    z_step(0, 3, 2)
    x1_step(1)
    z_step(0, 2, 2)
    y_step(0, 1, 0)
    x1_step(3)
    x0_step(7)
    y_step(0, 0, 0)
    x1_arrived(0)
    v_step(0, 0)
    v_step(0, 1)
    z_step(0, 0, 1)
    z_step(1, 0, 2)
    z_step(1, 1, 2)
    y_step(0, 3, 1)
    x1_step(4)
    y_step(1, 2, 1)
    y_step(0, 2, 2)
    z_step(1, 2, 2)
    x1_step(5)
    y_step(1, 3, 1)
    z_step(0, 1, 2)
    z_step(1, 3, 2)
    y_step(1, 0, 2)
    z_step(0, 3, 3)
    x1_step(6)
    y_step(0, 1, 1)
    z_step(0, 2, 3)
    y_step(1, 1, 2)
    x1_arrived(2)
    v_step(2, 0)
    y_step(0, 0, 1)
    v_step(2, 1)
    z_step(1, 0, 3)
    y_step(0, 3, 2)
    y_step(1, 2, 2)
    z_step(0, 0, 2)
    z_step(1, 1, 3)
    x1_arrived(1)
    v_step(1, 0)
    v_step(1, 1)
    y_step(0, 2, 3)
    z_step(0, 1, 3)
    y_step(1, 3, 2)
    z_step(1, 2, 3)
    y_step(1, 0, 3)
    z_step(1, 3, 3)
    y_step(0, 1, 2)
    y_step(1, 1, 3)
    x1_step(7)
    y_step(0, 0, 2)
    y_step(0, 3, 3)
    y_step(1, 2, 3)
    z_step(0, 0, 3)
    x1_arrived(4)
    v_step(4, 1)
    v_step(4, 0)
    x1_arrived(3)
    v_step(3, 0)
    y_step(1, 3, 3)
    v_step(3, 1)
    z2_step(2)
    y_step(0, 1, 3)
    z2_step(1)
    z2_step(3)
    y_step(0, 0, 3)
    y2_step(2)
    z2_step(0)
    x1_arrived(6)
    v_step(6, 1)
    x1_arrived(5)
    v_step(5, 0)
    y2_step(3)
    v_step(6, 0)
    v_step(5, 1)
    y2_step(1)
    y2_step(0)
    z3_step()
    x1_arrived(7)
    v_step(7, 0)
    v_step(7, 1)
    y3_step()
    finish(z_acc[0:SUB], z3r, r3sem.at[0], 0)
    finish(v_acc[0], v2r.at[0], r2sem.at[2], 256)
    finish(v_acc[1], v2r.at[1], r2sem.at[3], 384)
    finish(y_acc[Z - 1], y3r, r3sem.at[1], 128)

    g_swap(core).wait_send()

    @pl.loop(0, Z)
    def _(i):
        swap(i, core).wait_send()
        for way in range(2):
            x0_copy(way, i).wait_send()
            x1_copy(way, i).wait_send()

    for way in range(2):
        for k in range(4):
            for h in range(2):
                v_copy(way, k, h).wait_send()
            for j in range(X):
                if k > 0 or begins(way, j):
                    z_copy(way, j, k).wait_send()
                    y_copy(way, j, k).wait_send()
    for at, buf in enumerate((z2s, y2s, v2s.at[0], v2s.at[1])):
        drain(buf, s2sem.at[at])
    for at, buf in enumerate((z3s, y3s)):
        drain(buf, s3sem.at[at])


def per_device(activations, out_grads):
    def vm(*shape, dtype=BF16):
        return pltpu.VMEM(shape, dtype)

    dma = pltpu.SemaphoreType.DMA
    scratch = [
        vm(Z, CORES * TOK, WIDTH), vm(CORES * TOK, COLS), vm(BLOCK, BLOCK), vm(WIDTH, CORES * TOK),
        vm(Z, X, BLOCK, COLS, dtype=F32),
        vm(2, X, 4, BLOCK, 128), vm(2, X, 4, BLOCK, 128),
        vm(2, X, 4, Z, SUB, 128), vm(2, X, 4, Z, SUB, 128),
        vm(Z, 2, HALF, 256), vm(Z, 2, HALF, 256),
        vm(Z, 2, BLOCK, 256), vm(Z, 2, BLOCK, 256),
        vm(2, 4, 2, BLOCK, 128), vm(2, 4, 2, BLOCK, 128),
        vm(X - 1, BLOCK, 128), vm(X - 1, BLOCK, 128),
        vm(X - 1, Z, SUB, 128), vm(X - 1, Z, SUB, 128),
        vm(2, Y - 1, SUB, 128), vm(2, Y - 1, SUB, 128),
        vm(Y - 1, SUB, 128), vm(Y - 1, SUB, 128),
        vm(Z - 1, SUB, 128), vm(Z - 1, SUB, 128),
        vm(BLOCK, 128, dtype=F32), vm(Z, SUB, 128, dtype=F32), vm(2, SUB, 128, dtype=F32),
        dma((Z,)), dma, dma((Z,)), dma((Z,)), dma, dma,
        dma((2, X, 4)), dma((2, X, 4)), dma((2, X, 4)), dma((2, X, 4)),
        dma((Z, 2)), dma((Z, 2)), dma((Z, 2)), dma((Z, 2)), dma((2, 4, 2)), dma((2, 4, 2)),
        dma((4,)), dma((4,)), dma((2,)), dma((2,)),
    ]
    return pl.pallas_call(
        kernel,
        out_shape=jax.ShapeDtypeStruct((SUB, COLS), F32),
        in_specs=[pl.BlockSpec(memory_space=pl.ANY)] * 2,
        out_specs=pl.BlockSpec(memory_space=pltpu.VMEM),
        scratch_shapes=scratch,
        compiler_params=pltpu.CompilerParams(
            collective_id=0, has_side_effects=True, vmem_limit_bytes=60 * 1024 * 1024
        ),
        cost_estimate=pl.CostEstimate(
            flops=2 * CORES * TOK * Z * WIDTH * (COLS + BLOCK),
            bytes_accessed=TOK * (2 * Z * WIDTH + COLS) * 2,
            transcendentals=0,
        ),
    )(activations, out_grads)


def solution(mesh):
    return jax.shard_map(
        per_device,
        mesh=mesh,
        in_specs=(P(("narrow", "wide"), None), P(("narrow", "wide"), None)),
        out_specs=P(("narrow", "wide"), None),
        check_vma=False,
    )
```

```python
import math

import jax
import jax.numpy as jnp
from jax import lax
from jax.experimental import pallas as pl
from jax.experimental.pallas import tpu as pltpu
from jax.sharding import PartitionSpec as P

Z, CORES, X, Y = 8, 2, 4, 8
BLOCK = 128
HALF = BLOCK // 2
SUB = 16
TOK = 256
WIDTH = X * BLOCK
COLS = 512
F32, BF16 = jnp.float32, jnp.bfloat16
MESH = pl.DeviceIdType.MESH

OFFSET = (4, 3, 5, 2, 6, 1, 7, 0)
STEP = {offset: i for i, offset in enumerate(OFFSET)}
AHEAD = 3


def kernel(
    act_ref, grad_ref, out_ref,
    a_buf, g_buf, h_buf, t_buf, m_buf,
    zs, zr, ys, yr, xs0, xr0, xs1, xr1, vs0, vr0, vs, vr,
    z2s, z2r, y2s, y2r, v2s, v2r, z3s, z3r, y3s, y3r,
    z_acc, y_acc, v_acc,
    load_sem, gload_sem, asend, arecv, gsend, grecv,
    zssem, zrsem, yssem, yrsem, x0ssem, x0rsem, x1ssem, x1rsem, v0ssem, vssem, vrsem,
    s2sem, r2sem, s3sem, r3sem,
):
    n = lax.axis_index("narrow")
    w = lax.axis_index("wide")
    z, core = n // CORES, n % CORES
    x, y = w // Y, w % Y
    other = 1 - core

    def at_z(d):
        return (((z + d + Z) % Z) * CORES + core, w)

    def at_y(d):
        return (n, x * Y + (y + d + Y) % Y)

    def at_x(d):
        return (n, ((x + d + X) % X) * Y + y)

    sibling = (z * CORES + other, w)

    def remote(src, dst, ssem, rsem, target):
        return pltpu.make_async_remote_copy(
            src_ref=src, dst_ref=dst, send_sem=ssem, recv_sem=rsem,
            device_id=target, device_id_type=MESH,
        )

    def drain(buf, sem):
        pltpu.make_async_copy(buf, buf, sem).wait()

    def place(i):
        return (z + 4 + i // 2 - (i % 2) * i + 2 * Z) % Z

    def own_load(i):
        return pltpu.make_async_copy(
            act_ref.at[:, pl.ds((place(i) * CORES + core) * WIDTH, WIDTH)],
            a_buf.at[i, pl.ds(core * TOK, TOK), :],
            load_sem,
        )

    def swap(i, half):
        return remote(
            act_ref.at[:, pl.ds((place(i) * CORES + other) * WIDTH, WIDTH)],
            a_buf.at[i, pl.ds(half * TOK, TOK), :],
            asend, arecv.at[i], sibling,
        )

    def g_swap(half):
        return remote(grad_ref, g_buf.at[pl.ds(half * TOK, TOK), :], gsend, grecv, sibling)

    g_load = pltpu.make_async_copy(grad_ref, g_buf.at[pl.ds(core * TOK, TOK), :], gload_sem)

    barrier = pltpu.get_barrier_semaphore()
    pl.semaphore_signal(barrier, inc=1, device_id=sibling, device_id_type=MESH)
    for d in range(1, Z):
        pl.semaphore_signal(barrier, inc=1, device_id=at_z(d), device_id_type=MESH)
    for d in range(1, Y):
        pl.semaphore_signal(barrier, inc=1, device_id=at_y(d), device_id_type=MESH)
    for d in range(1, X):
        pl.semaphore_signal(barrier, inc=1, device_id=at_x(d), device_id_type=MESH)

    g_load.start()

    @pl.loop(0, Z)
    def _(i):
        own_load(i).start()

    row = (lax.broadcasted_iota(jnp.int32, (BLOCK, BLOCK), 0) + y * SUB) & (BLOCK - 1)
    col = lax.broadcasted_iota(jnp.int32, (BLOCK, BLOCK), 1)
    bits = row & col
    bits = bits ^ (bits >> 4)
    bits = bits ^ (bits >> 2)
    bits = bits ^ (bits >> 1)
    h_buf[...] = (1 - 2 * (bits & 1)).astype(F32).astype(BF16)

    pl.semaphore_wait(barrier, 1 + (Z - 1) + (Y - 1) + (X - 1))

    g_swap(core).start()

    for i in range(AHEAD):
        swap(i, core).start()

    def compute(i):
        swap(i, other).wait_recv()
        if i + AHEAD < Z:
            swap(i + AHEAD, core).start()
        for j in range(X):
            b = (x + j) % X
            t_buf[j * BLOCK : (j + 1) * BLOCK] = lax.dot_general(
                h_buf[...],
                a_buf[i, :, pl.ds(pl.multiple_of(b * BLOCK, BLOCK), BLOCK)],
                (((1,), (1,)), ((), ())),
                preferred_element_type=F32,
            ).astype(BF16)
        m_buf[i] = jnp.dot(t_buf[...], g_buf[...], preferred_element_type=F32).reshape(X, BLOCK, COLS)

    def way_sign(way):
        return 1 - 2 * way

    def slot(way, j, k):
        if k == 0:
            return 24 + 2 * way + j % 2
        if k == 3:
            return 16 + 2 * j + way
        return 8 * (k - 1) + 4 * way + j

    def mark(way, j, k):
        return 16 + j if k == 3 else slot(way, j, k) - 4 * (k == 0)

    def z_copy(way, j, k):
        return remote(
            zs.at[slot(way, j, k)], zr.at[slot(way, j, k)], zssem, zrsem.at[mark(way, j, k)],
            at_z(way_sign(way)),
        )

    def begins(way, j):
        return j // 2 == way

    def z_step(way, j, k):
        i = STEP[(way_sign(way) * (4 - k)) % Z]
        part = m_buf[i, j, :, 0:128]
        if k >= 2 or (k == 1 and begins(way, j)):
            z_copy(way, j, k - 1).wait_recv()
            part = part + zr[slot(way, j, k - 1)].astype(F32)
        zs[slot(way, j, k)] = part.astype(BF16)
        z_copy(way, j, k).start()

    def y_copy(way, j, k):
        return remote(
            ys.at[slot(way, j, k)], yr.at[slot(way, j, k)], yssem, yrsem.at[mark(way, j, k)],
            at_y(way_sign(way)),
        )

    def y_step(way, j, k):
        first = ((way_sign(way) * (4 - k)) % Y) * SUB
        part = m_buf[:, j, first : first + SUB, 128:256]
        if k >= 2 or (k == 1 and begins(way, j)):
            y_copy(way, j, k - 1).wait_recv()
            part = part + yr[slot(way, j, k - 1)].astype(F32)
        ys[slot(way, j, k)] = part.astype(BF16)
        y_copy(way, j, k).start()

    def x0_copy(way, i):
        return remote(
            xs0.at[i, way], xr0.at[i, way], x0ssem, x0rsem.at[i],
            at_x(way_sign(way)),
        )

    def x1_copy(way, i):
        return remote(
            xs1.at[i, way], xr1.at[i, way], x1ssem, x1rsem.at[i],
            at_x(way_sign(way)),
        )

    def v_slot(way, k, h):
        return 8 + 2 * h + way if k == 3 else 4 * (k - 1) + 2 * way + h

    def v_copy(way, k, h):
        if k == 0:
            src, dst, ssem, mine = vs0.at[way, h], vr0.at[way, h], v0ssem, 10 + 2 * way + h
        else:
            at = v_slot(way, k, h)
            src, dst, ssem, mine = vs.at[at], vr.at[at], vssem, 8 + h if k == 3 else at
        return remote(src, dst, ssem, vrsem.at[mine], at_z(way_sign(way)))

    def w_copy(j, h):
        return remote(
            v2s.at[h, j - 1], v2r.at[h, j - 1], s2sem.at[2 + h], r2sem.at[2 + h], at_y(j)
        )

    def x0_step(i):
        for way in range(2):
            xs0[i, way] = m_buf[i, 2, way * HALF : (way + 1) * HALF, 256:512].astype(BF16)
            x0_copy(way, i).start()

    def x1_step(i):
        drain(xr0.at[i], x0rsem.at[i])
        for way in range(2):
            j = 1 + 2 * way
            mine = slice(way * HALF, (way + 1) * HALF)
            rest = slice((1 - way) * HALF, (2 - way) * HALF)
            xs1[i, way, mine] = (m_buf[i, j, mine, 256:512] + xr0[i, way].astype(F32)).astype(BF16)
            xs1[i, way, rest] = m_buf[i, j, rest, 256:512].astype(BF16)
            x1_copy(way, i).start()

    def x2_rows(i, rows, h):
        there = slice(h * 128, (h + 1) * 128)
        return (
            m_buf[i, 0, rows, 256 + h * 128 : 384 + h * 128]
            + xr1[i, 0, rows, there].astype(F32)
            + xr1[i, 1, rows, there].astype(F32)
        )

    def v_step(i, h):
        if i == 0:
            for way in range(2):
                rows = slice(way * HALF, (way + 1) * HALF)
                vs0[way, h] = x2_rows(0, rows, h).astype(BF16)
                v_copy(way, 0, h).start()
            return
        if i < Z - 1:
            way, k = 1 - i % 2, (i + 1) // 2
            v_copy(way, k - 1, h).wait_recv()
            if k == 1:
                mine = slice(way * HALF, (way + 1) * HALF)
                rest = slice((1 - way) * HALF, (2 - way) * HALF)
                vs[v_slot(way, 1, h), mine] = (
                    x2_rows(i, mine, h) + vr0[way, h].astype(F32)
                ).astype(BF16)
                vs[v_slot(way, 1, h), rest] = x2_rows(i, rest, h).astype(BF16)
            else:
                vs[v_slot(way, k, h)] = (
                    x2_rows(i, slice(0, BLOCK), h) + vr[v_slot(way, k - 1, h)].astype(F32)
                ).astype(BF16)
            v_copy(way, k, h).start()
            return
        drain(vr.at[pl.ds(8 + 2 * h, 2)], vrsem.at[8 + h])
        part = (
            x2_rows(i, slice(0, BLOCK), h) + vr[8 + 2 * h].astype(F32) + vr[9 + 2 * h].astype(F32)
        )
        v_acc[h] = part[0:SUB]
        for j in range(1, Y):
            v2s[h, j - 1] = part[j * SUB : (j + 1) * SUB].astype(BF16)
            w_copy(j, h).start()

    def x1_arrived(i):
        drain(xr1.at[i], x1rsem.at[i])

    def z2_step(j):
        drain(zr.at[pl.ds(slot(0, j, 3), 2)], zrsem.at[mark(0, j, 3)])
        part = m_buf[Z - 1, j, :, 0:128] + zr[slot(0, j, 3)].astype(F32) + zr[slot(1, j, 3)].astype(F32)
        if j == 0:
            z_acc[...] = part
        else:
            z2s[j - 1] = part.astype(BF16)
            remote(z2s.at[j - 1], z2r.at[j - 1], s2sem.at[0], r2sem.at[0], at_x(j)).start()

    def y2_step(j):
        drain(yr.at[pl.ds(slot(0, j, 3), 2)], yrsem.at[mark(0, j, 3)])
        part = m_buf[:, j, 0:SUB, 128:256] + yr[slot(0, j, 3)].astype(F32) + yr[slot(1, j, 3)].astype(F32)
        if j == 0:
            y_acc[...] = part
        else:
            y2s[j - 1] = part.astype(BF16)
            remote(y2s.at[j - 1], y2r.at[j - 1], s2sem.at[1], r2sem.at[1], at_x(j)).start()

    def z3_step():
        drain(z2r, r2sem.at[0])
        part = z_acc[...]
        for q in range(X - 1):
            part = part + z2r[q].astype(F32)
        z_acc[...] = part
        for j in range(1, Y):
            z3s[j - 1] = part[j * SUB : (j + 1) * SUB].astype(BF16)
            remote(z3s.at[j - 1], z3r.at[j - 1], s3sem.at[0], r3sem.at[0], at_y(j)).start()

    def y3_step():
        drain(y2r, r2sem.at[1])
        part = y_acc[...]
        for q in range(X - 1):
            part = part + y2r[q].astype(F32)
        y_acc[...] = part
        for j in range(1, Z):
            y3s[j - 1] = part[STEP[j]].astype(BF16)
            remote(y3s.at[j - 1], y3r.at[j - 1], s3sem.at[1], r3sem.at[1], at_z(j)).start()

    scale = 1.0 / (Z * CORES * X * Y * math.sqrt(BLOCK))

    def finish(own, received, sem, first):
        drain(received, sem)
        total = own
        for q in range(received.shape[0]):
            total = total + received[q].astype(F32)
        out_ref[:, first : first + 128] = total * scale

    g_load.wait()
    drain(a_buf.at[:, pl.ds(core * TOK, TOK), :], load_sem)
    g_swap(other).wait_recv()

    compute(0)
    x0_step(0)
    compute(1)
    x0_step(1)
    compute(2)
    x0_step(2)
    z_step(1, 2, 0)
    compute(3)
    x0_step(3)
    z_step(0, 1, 0)
    z_step(1, 3, 0)
    compute(4)
    x0_step(4)
    compute(5)
    z_step(0, 2, 1)
    x0_step(5)
    compute(6)
    x1_step(0)
    compute(7)
    y_step(1, 2, 0)
    y_step(0, 1, 0)
    z_step(0, 3, 1)
    z_step(1, 1, 1)
    y_step(0, 0, 0)
    x1_step(1)
    y_step(0, 3, 1)
    y_step(1, 3, 0)
    z_step(1, 2, 1)
    y_step(1, 1, 1)
    z_step(0, 0, 0)
    x1_step(2)
    z_step(0, 1, 1)
    z_step(1, 3, 1)
    x0_step(6)
    z_step(1, 0, 1)
    y_step(0, 2, 1)
    z_step(0, 2, 2)
    y_step(1, 0, 1)
    x0_step(7)
    y_step(1, 2, 1)
    x1_arrived(0)
    v_step(0, 1)
    v_step(0, 0)
    y_step(0, 1, 1)
    z_step(0, 3, 2)
    z_step(1, 1, 2)
    y_step(1, 3, 1)
    z_step(1, 2, 2)
    z_step(0, 0, 1)
    x1_step(4)
    y_step(0, 0, 1)
    y_step(1, 1, 2)
    z_step(0, 1, 2)
    z_step(1, 3, 2)
    y_step(0, 3, 2)
    y_step(0, 2, 2)
    x1_step(3)
    z_step(0, 2, 3)
    z_step(1, 0, 2)
    x1_arrived(1)
    v_step(1, 1)
    x1_arrived(2)
    v_step(2, 1)
    y_step(1, 2, 2)
    v_step(2, 0)
    x1_step(5)
    v_step(1, 0)
    y_step(0, 1, 2)
    y_step(1, 3, 2)
    z_step(0, 3, 3)
    z_step(1, 2, 3)
    y_step(1, 0, 2)
    z_step(0, 0, 2)
    z_step(1, 1, 3)
    x1_step(6)
    z_step(1, 3, 3)
    z_step(0, 1, 3)
    y_step(1, 1, 3)
    y_step(0, 3, 3)
    x1_step(7)
    y_step(0, 2, 3)
    y_step(1, 2, 3)
    x1_arrived(3)
    v_step(3, 1)
    x1_arrived(4)
    v_step(4, 1)
    y_step(0, 0, 2)
    v_step(4, 0)
    v_step(3, 0)
    y_step(0, 1, 3)
    y_step(1, 3, 3)
    z2_step(2)
    z_step(1, 0, 3)
    z_step(0, 0, 3)
    z2_step(1)
    z2_step(3)
    y_step(1, 0, 3)
    y2_step(2)
    x1_arrived(5)
    v_step(5, 1)
    x1_arrived(6)
    v_step(6, 1)
    v_step(5, 0)
    y_step(0, 0, 3)
    v_step(6, 0)
    y2_step(1)
    y2_step(3)
    z2_step(0)
    z3_step()
    x1_arrived(7)
    v_step(7, 1)
    y2_step(0)
    v_step(7, 0)
    y3_step()
    finish(z_acc[0:SUB], z3r, r3sem.at[0], 0)
    finish(y_acc[Z - 1], y3r, r3sem.at[1], 128)
    finish(v_acc[0], v2r.at[0], r2sem.at[2], 256)
    finish(v_acc[1], v2r.at[1], r2sem.at[3], 384)

    g_swap(core).wait_send()

    drain(a_buf.at[:, pl.ds(0, TOK), :], asend)
    for buf, sem in (
        (zs, zssem), (ys, yssem), (xs0, x0ssem), (xs1, x1ssem), (vs0, v0ssem), (vs, vssem)
    ):
        drain(buf, sem)
    for at, buf in enumerate((z2s, y2s, v2s.at[0], v2s.at[1])):
        drain(buf, s2sem.at[at])
    for at, buf in enumerate((z3s, y3s)):
        drain(buf, s3sem.at[at])


def per_device(activations, out_grads):
    def vm(*shape, dtype=BF16):
        return pltpu.VMEM(shape, dtype)

    dma = pltpu.SemaphoreType.DMA
    scratch = [
        vm(Z, CORES * TOK, WIDTH), vm(CORES * TOK, COLS), vm(BLOCK, BLOCK), vm(WIDTH, CORES * TOK),
        vm(Z, X, BLOCK, COLS, dtype=F32),
        vm(28, BLOCK, 128), vm(28, BLOCK, 128),
        vm(28, Z, SUB, 128), vm(28, Z, SUB, 128),
        vm(Z, 2, HALF, 256), vm(Z, 2, HALF, 256),
        vm(Z, 2, BLOCK, 256), vm(Z, 2, BLOCK, 256),
        vm(2, 2, HALF, 128), vm(2, 2, HALF, 128),
        vm(12, BLOCK, 128), vm(12, BLOCK, 128),
        vm(X - 1, BLOCK, 128), vm(X - 1, BLOCK, 128),
        vm(X - 1, Z, SUB, 128), vm(X - 1, Z, SUB, 128),
        vm(2, Y - 1, SUB, 128), vm(2, Y - 1, SUB, 128),
        vm(Y - 1, SUB, 128), vm(Y - 1, SUB, 128),
        vm(Z - 1, SUB, 128), vm(Z - 1, SUB, 128),
        vm(BLOCK, 128, dtype=F32), vm(Z, SUB, 128, dtype=F32), vm(2, SUB, 128, dtype=F32),
        dma, dma, dma, dma((Z,)), dma, dma,
        dma, dma((24,)), dma, dma((24,)),
        dma, dma((Z,)), dma, dma((Z,)), dma, dma, dma((14,)),
        dma((4,)), dma((4,)), dma((2,)), dma((2,)),
    ]
    return pl.pallas_call(
        kernel,
        out_shape=jax.ShapeDtypeStruct((SUB, COLS), F32),
        in_specs=[pl.BlockSpec(memory_space=pl.ANY)] * 2,
        out_specs=pl.BlockSpec(memory_space=pltpu.VMEM),
        scratch_shapes=scratch,
        compiler_params=pltpu.CompilerParams(
            collective_id=0, has_side_effects=True, vmem_limit_bytes=60 * 1024 * 1024
        ),
        cost_estimate=pl.CostEstimate(
            flops=2 * CORES * TOK * Z * WIDTH * (COLS + BLOCK),
            bytes_accessed=TOK * (2 * Z * WIDTH + COLS) * 2,
            transcendentals=0,
        ),
    )(activations, out_grads)


def solution(mesh):
    return jax.shard_map(
        per_device,
        mesh=mesh,
        in_specs=(P(("narrow", "wide"), None), P(("narrow", "wide"), None)),
        out_specs=P(("narrow", "wide"), None),
        check_vma=False,
    )
```

```python
import math

import jax
import jax.numpy as jnp
from jax import lax
from jax.experimental import pallas as pl
from jax.experimental.pallas import tpu as pltpu
from jax.sharding import PartitionSpec as P

Z, CORES, X, Y = 8, 2, 4, 8
BLOCK = 128
HALF = BLOCK // 2
SUB = 16
TOK = 256
WIDTH = X * BLOCK
COLS = 512
F32, BF16 = jnp.float32, jnp.bfloat16
MESH = pl.DeviceIdType.MESH

OFFSET = (4, 3, 5, 2, 6, 1, 7, 0)
STEP = {offset: i for i, offset in enumerate(OFFSET)}
AHEAD = 3


def kernel(
    act_ref, grad_ref, out_ref,
    a_buf, g_buf, h_buf, t_buf, m_buf,
    zs, zr, ys, yr, xs0, xr0, xs1, xr1, vs0, vr0, vs, vr,
    z2s, z2r, y2s, y2r, v2s, v2r, z3s, z3r, y3s, y3r,
    z_acc, y_acc, v_acc,
    load_sem, gload_sem, asend, arecv, gsend, grecv,
    zssem, zrsem, yssem, yrsem, x0ssem, x0rsem, x1ssem, x1rsem, v0ssem, vssem, vrsem,
    s2sem, r2sem, s3sem, r3sem,
):
    n = lax.axis_index("narrow")
    w = lax.axis_index("wide")
    z, core = n // CORES, n % CORES
    x, y = w // Y, w % Y
    other = 1 - core

    def at_z(d):
        return (((z + d + Z) % Z) * CORES + core, w)

    def at_y(d):
        return (n, x * Y + (y + d + Y) % Y)

    def at_x(d):
        return (n, ((x + d + X) % X) * Y + y)

    sibling = (z * CORES + other, w)

    def remote(src, dst, ssem, rsem, target):
        return pltpu.make_async_remote_copy(
            src_ref=src, dst_ref=dst, send_sem=ssem, recv_sem=rsem,
            device_id=target, device_id_type=MESH,
        )

    def drain(buf, sem):
        pltpu.make_async_copy(buf, buf, sem).wait()

    def place(i):
        return (z + 4 + i // 2 - (i % 2) * i + 2 * Z) % Z

    def own_load(i):
        return pltpu.make_async_copy(
            act_ref.at[:, pl.ds((place(i) * CORES + core) * WIDTH, WIDTH)],
            a_buf.at[i, pl.ds(core * TOK, TOK), :],
            load_sem,
        )

    def swap(i, half):
        return remote(
            act_ref.at[:, pl.ds((place(i) * CORES + other) * WIDTH, WIDTH)],
            a_buf.at[i, pl.ds(half * TOK, TOK), :],
            asend, arecv.at[i + X - 1], sibling,
        )

    def columns(j):
        return pl.multiple_of((x + j) % X * BLOCK, BLOCK)

    def first_swap(j, half):
        return remote(
            act_ref.at[:, pl.ds((place(0) * CORES + other) * WIDTH + columns(j), BLOCK)],
            a_buf.at[0, pl.ds(half * TOK, TOK), pl.ds(columns(j), BLOCK)],
            asend, arecv.at[j], sibling,
        )

    def g_swap(part, half):
        there = pl.ds(part * (COLS // 2), COLS // 2)
        return remote(
            grad_ref.at[:, there], g_buf.at[pl.ds(half * TOK, TOK), there],
            gsend, grecv.at[part], sibling,
        )

    g_load = pltpu.make_async_copy(grad_ref, g_buf.at[pl.ds(core * TOK, TOK), :], gload_sem)

    barrier = pltpu.get_barrier_semaphore()
    pl.semaphore_signal(barrier, inc=1, device_id=sibling, device_id_type=MESH)
    for d in range(1, Z):
        pl.semaphore_signal(barrier, inc=1, device_id=at_z(d), device_id_type=MESH)
    for d in range(1, Y):
        pl.semaphore_signal(barrier, inc=1, device_id=at_y(d), device_id_type=MESH)
    for d in range(1, X):
        pl.semaphore_signal(barrier, inc=1, device_id=at_x(d), device_id_type=MESH)

    g_load.start()

    @pl.loop(0, Z)
    def _(i):
        own_load(i).start()

    row = (lax.broadcasted_iota(jnp.int32, (BLOCK, BLOCK), 0) + y * SUB) & (BLOCK - 1)
    col = lax.broadcasted_iota(jnp.int32, (BLOCK, BLOCK), 1)
    bits = row & col
    bits = bits ^ (bits >> 4)
    bits = bits ^ (bits >> 2)
    bits = bits ^ (bits >> 1)
    h_buf[...] = (1 - 2 * (bits & 1)).astype(F32).astype(BF16)

    pl.semaphore_wait(barrier, 1 + (Z - 1) + (Y - 1) + (X - 1))

    g_swap(1, core).start()
    for j in (2, 0, 1, 3):
        first_swap(j, core).start()
    g_swap(0, core).start()
    for i in range(1, AHEAD):
        swap(i, core).start()

    def turn(i, j):
        t_buf[j * BLOCK : (j + 1) * BLOCK] = lax.dot_general(
            h_buf[...],
            a_buf[i, :, pl.ds(columns(j), BLOCK)],
            (((1,), (1,)), ((), ())),
            preferred_element_type=F32,
        ).astype(BF16)

    def compute_first():
        g_load.wait()
        drain(a_buf.at[:, pl.ds(core * TOK, TOK), :], load_sem)
        g_swap(1, other).wait_recv()
        first_swap(2, other).wait_recv()
        turn(0, 2)
        m_buf[0, 2, :, 256:512] = jnp.dot(
            t_buf[2 * BLOCK : 3 * BLOCK], g_buf[:, 256:512], preferred_element_type=F32
        )

    def compute(i):
        if i == 0:
            for j in (0, 1, 3):
                first_swap(j, other).wait_recv()
            g_swap(0, other).wait_recv()
        else:
            swap(i, other).wait_recv()
        if i + AHEAD < Z:
            swap(i + AHEAD, core).start()
        for j in range(X):
            if i > 0 or j != 2:
                turn(i, j)
        m_buf[i] = jnp.dot(t_buf[...], g_buf[...], preferred_element_type=F32).reshape(X, BLOCK, COLS)

    def way_sign(way):
        return 1 - 2 * way

    def slot(way, j, k):
        if k == 0:
            return 24 + 2 * way + j % 2
        if k == 3:
            return 16 + 2 * j + way
        return 8 * (k - 1) + 4 * way + j

    def mark(way, j, k):
        return 16 + j if k == 3 else slot(way, j, k) - 4 * (k == 0)

    def z_copy(way, j, k):
        return remote(
            zs.at[slot(way, j, k)], zr.at[slot(way, j, k)], zssem, zrsem.at[mark(way, j, k)],
            at_z(way_sign(way)),
        )

    def begins(way, j):
        return j // 2 == way

    def z_step(way, j, k):
        i = STEP[(way_sign(way) * (4 - k)) % Z]
        part = m_buf[i, j, :, 0:128]
        if k >= 2 or (k == 1 and begins(way, j)):
            z_copy(way, j, k - 1).wait_recv()
            part = part + zr[slot(way, j, k - 1)].astype(F32)
        zs[slot(way, j, k)] = part.astype(BF16)
        z_copy(way, j, k).start()

    def y_copy(way, j, k):
        return remote(
            ys.at[slot(way, j, k)], yr.at[slot(way, j, k)], yssem, yrsem.at[mark(way, j, k)],
            at_y(way_sign(way)),
        )

    def y_step(way, j, k):
        first = ((way_sign(way) * (4 - k)) % Y) * SUB
        part = m_buf[:, j, first : first + SUB, 128:256]
        if k >= 2 or (k == 1 and begins(way, j)):
            y_copy(way, j, k - 1).wait_recv()
            part = part + yr[slot(way, j, k - 1)].astype(F32)
        ys[slot(way, j, k)] = part.astype(BF16)
        y_copy(way, j, k).start()

    def x0_copy(way, i):
        return remote(
            xs0.at[i, way], xr0.at[i, way], x0ssem, x0rsem.at[i],
            at_x(way_sign(way)),
        )

    def x1_copy(way, i):
        return remote(
            xs1.at[i, way], xr1.at[i, way], x1ssem, x1rsem.at[i],
            at_x(way_sign(way)),
        )

    def v_slot(way, k, h):
        return 8 + 2 * h + way if k == 3 else 4 * (k - 1) + 2 * way + h

    def v_copy(way, k, h):
        if k == 0:
            src, dst, ssem, mine = vs0.at[way, h], vr0.at[way, h], v0ssem, 10 + 2 * way + h
        else:
            at = v_slot(way, k, h)
            src, dst, ssem, mine = vs.at[at], vr.at[at], vssem, 8 + h if k == 3 else at
        return remote(src, dst, ssem, vrsem.at[mine], at_z(way_sign(way)))

    def w_copy(j, h):
        return remote(
            v2s.at[h, j - 1], v2r.at[h, j - 1], s2sem.at[2 + h], r2sem.at[2 + h], at_y(j)
        )

    def x0_step(i):
        for way in range(2):
            xs0[i, way] = m_buf[i, 2, way * HALF : (way + 1) * HALF, 256:512].astype(BF16)
            x0_copy(way, i).start()

    def x1_step(i):
        drain(xr0.at[i], x0rsem.at[i])
        for way in range(2):
            j = 1 + 2 * way
            mine = slice(way * HALF, (way + 1) * HALF)
            rest = slice((1 - way) * HALF, (2 - way) * HALF)
            xs1[i, way, mine] = (m_buf[i, j, mine, 256:512] + xr0[i, way].astype(F32)).astype(BF16)
            xs1[i, way, rest] = m_buf[i, j, rest, 256:512].astype(BF16)
            x1_copy(way, i).start()

    def x2_rows(i, rows, h):
        there = slice(h * 128, (h + 1) * 128)
        return (
            m_buf[i, 0, rows, 256 + h * 128 : 384 + h * 128]
            + xr1[i, 0, rows, there].astype(F32)
            + xr1[i, 1, rows, there].astype(F32)
        )

    def v_step(i, h):
        if i == 0:
            for way in range(2):
                rows = slice(way * HALF, (way + 1) * HALF)
                vs0[way, h] = x2_rows(0, rows, h).astype(BF16)
                v_copy(way, 0, h).start()
            return
        if i < Z - 1:
            way, k = 1 - i % 2, (i + 1) // 2
            v_copy(way, k - 1, h).wait_recv()
            if k == 1:
                mine = slice(way * HALF, (way + 1) * HALF)
                rest = slice((1 - way) * HALF, (2 - way) * HALF)
                vs[v_slot(way, 1, h), mine] = (
                    x2_rows(i, mine, h) + vr0[way, h].astype(F32)
                ).astype(BF16)
                vs[v_slot(way, 1, h), rest] = x2_rows(i, rest, h).astype(BF16)
            else:
                vs[v_slot(way, k, h)] = (
                    x2_rows(i, slice(0, BLOCK), h) + vr[v_slot(way, k - 1, h)].astype(F32)
                ).astype(BF16)
            v_copy(way, k, h).start()
            return
        drain(vr.at[pl.ds(8 + 2 * h, 2)], vrsem.at[8 + h])
        part = (
            x2_rows(i, slice(0, BLOCK), h) + vr[8 + 2 * h].astype(F32) + vr[9 + 2 * h].astype(F32)
        )
        v_acc[h] = part[0:SUB]
        for j in OFFSET[:-1]:
            v2s[h, j - 1] = part[j * SUB : (j + 1) * SUB].astype(BF16)
            w_copy(j, h).start()

    def x1_arrived(i):
        drain(xr1.at[i], x1rsem.at[i])

    def z2_step(j):
        drain(zr.at[pl.ds(slot(0, j, 3), 2)], zrsem.at[mark(0, j, 3)])
        part = m_buf[Z - 1, j, :, 0:128] + zr[slot(0, j, 3)].astype(F32) + zr[slot(1, j, 3)].astype(F32)
        if j == 0:
            z_acc[...] = part
        else:
            z2s[j - 1] = part.astype(BF16)
            remote(z2s.at[j - 1], z2r.at[j - 1], s2sem.at[0], r2sem.at[0], at_x(j)).start()

    def y2_step(j):
        drain(yr.at[pl.ds(slot(0, j, 3), 2)], yrsem.at[mark(0, j, 3)])
        part = m_buf[:, j, 0:SUB, 128:256] + yr[slot(0, j, 3)].astype(F32) + yr[slot(1, j, 3)].astype(F32)
        if j == 0:
            y_acc[...] = part
        else:
            y2s[j - 1] = part.astype(BF16)
            remote(y2s.at[j - 1], y2r.at[j - 1], s2sem.at[1], r2sem.at[1], at_x(j)).start()

    def z3_step():
        drain(z2r, r2sem.at[0])
        part = z_acc[...]
        for q in range(X - 1):
            part = part + z2r[q].astype(F32)
        z_acc[...] = part
        for j in OFFSET[:-1]:
            z3s[j - 1] = part[j * SUB : (j + 1) * SUB].astype(BF16)
            remote(z3s.at[j - 1], z3r.at[j - 1], s3sem.at[0], r3sem.at[0], at_y(j)).start()

    def y3_step():
        drain(y2r, r2sem.at[1])
        part = y_acc[...]
        for q in range(X - 1):
            part = part + y2r[q].astype(F32)
        y_acc[...] = part
        for j in OFFSET[:-1]:
            y3s[j - 1] = part[STEP[j]].astype(BF16)
            remote(y3s.at[j - 1], y3r.at[j - 1], s3sem.at[1], r3sem.at[1], at_z(j)).start()

    scale = 1.0 / (Z * CORES * X * Y * math.sqrt(BLOCK))

    def finish(own, received, sem, first):
        drain(received, sem)
        total = own
        for q in range(received.shape[0]):
            total = total + received[q].astype(F32)
        out_ref[:, first : first + 128] = total * scale


    compute_first()
    x0_step(0)
    compute(0)
    compute(1)
    x0_step(1)
    compute(2)
    x0_step(2)
    z_step(1, 2, 0)
    compute(3)
    x0_step(3)
    z_step(0, 1, 0)
    compute(4)
    x0_step(4)
    z_step(1, 3, 0)
    x1_step(0)
    compute(5)
    compute(6)
    compute(7)
    y_step(1, 2, 0)
    x0_step(6)
    z_step(0, 0, 0)
    y_step(0, 1, 0)
    z_step(1, 1, 1)
    y_step(1, 3, 0)
    x1_step(2)
    z_step(0, 2, 1)
    y_step(1, 1, 1)
    z_step(1, 2, 1)
    y_step(0, 0, 0)
    z_step(1, 0, 1)
    y_step(0, 2, 1)
    z_step(0, 1, 1)
    y_step(1, 0, 1)
    z_step(1, 3, 1)
    x1_step(1)
    x0_step(5)
    z_step(0, 3, 1)
    y_step(0, 3, 1)
    x1_step(4)
    x1_arrived(0)
    v_step(0, 1)
    v_step(0, 0)
    x0_step(7)
    y_step(1, 2, 1)
    z_step(0, 0, 1)
    z_step(1, 1, 2)
    y_step(0, 1, 1)
    y_step(1, 3, 1)
    z_step(0, 2, 2)
    z_step(1, 2, 2)
    x1_step(3)
    y_step(1, 1, 2)
    z_step(0, 1, 2)
    z_step(1, 0, 2)
    y_step(0, 0, 1)
    y_step(0, 2, 2)
    z_step(0, 3, 2)
    x1_step(6)
    z_step(1, 3, 2)
    y_step(1, 0, 2)
    x1_arrived(2)
    v_step(2, 1)
    x1_arrived(1)
    v_step(1, 0)
    y_step(1, 2, 2)
    v_step(1, 1)
    v_step(2, 0)
    x1_step(5)
    y_step(0, 3, 2)
    y_step(1, 3, 2)
    z_step(0, 2, 3)
    y_step(0, 1, 2)
    z_step(1, 2, 3)
    z_step(0, 1, 3)
    z_step(1, 1, 3)
    y_step(1, 1, 3)
    y_step(0, 0, 2)
    z_step(0, 0, 2)
    z_step(0, 3, 3)
    z_step(1, 3, 3)
    y_step(0, 2, 3)
    x1_step(7)
    x1_arrived(4)
    v_step(4, 1)
    y_step(1, 2, 3)
    x1_arrived(3)
    v_step(3, 1)
    v_step(3, 0)
    y_step(0, 3, 3)
    v_step(4, 0)
    y_step(1, 3, 3)
    y_step(1, 0, 3)
    y_step(0, 1, 3)
    z2_step(2)
    z2_step(1)
    z_step(1, 0, 3)
    y_step(0, 0, 3)
    z_step(0, 0, 3)
    z2_step(3)
    x1_arrived(6)
    v_step(6, 1)
    y2_step(2)
    x1_arrived(5)
    v_step(5, 1)
    v_step(6, 0)
    y2_step(3)
    v_step(5, 0)
    y2_step(1)
    y2_step(0)
    z2_step(0)
    z3_step()
    x1_arrived(7)
    v_step(7, 1)
    v_step(7, 0)
    y3_step()
    finish(v_acc[1], v2r.at[1], r2sem.at[3], 384)
    finish(z_acc[0:SUB], z3r, r3sem.at[0], 0)
    finish(v_acc[0], v2r.at[0], r2sem.at[2], 256)
    finish(y_acc[Z - 1], y3r, r3sem.at[1], 128)

    drain(g_buf.at[pl.ds(0, TOK), :], gsend)

    drain(a_buf.at[:, pl.ds(0, TOK), :], asend)
    for buf, sem in (
        (zs, zssem), (ys, yssem), (xs0, x0ssem), (xs1, x1ssem), (vs0, v0ssem), (vs, vssem)
    ):
        drain(buf, sem)
    for at, buf in enumerate((z2s, y2s, v2s.at[0], v2s.at[1])):
        drain(buf, s2sem.at[at])
    for at, buf in enumerate((z3s, y3s)):
        drain(buf, s3sem.at[at])


def per_device(activations, out_grads):
    def vm(*shape, dtype=BF16):
        return pltpu.VMEM(shape, dtype)

    dma = pltpu.SemaphoreType.DMA
    scratch = [
        vm(Z, CORES * TOK, WIDTH), vm(CORES * TOK, COLS), vm(BLOCK, BLOCK), vm(WIDTH, CORES * TOK),
        vm(Z, X, BLOCK, COLS, dtype=F32),
        vm(28, BLOCK, 128), vm(28, BLOCK, 128),
        vm(28, Z, SUB, 128), vm(28, Z, SUB, 128),
        vm(Z, 2, HALF, 256), vm(Z, 2, HALF, 256),
        vm(Z, 2, BLOCK, 256), vm(Z, 2, BLOCK, 256),
        vm(2, 2, HALF, 128), vm(2, 2, HALF, 128),
        vm(12, BLOCK, 128), vm(12, BLOCK, 128),
        vm(X - 1, BLOCK, 128), vm(X - 1, BLOCK, 128),
        vm(X - 1, Z, SUB, 128), vm(X - 1, Z, SUB, 128),
        vm(2, Y - 1, SUB, 128), vm(2, Y - 1, SUB, 128),
        vm(Y - 1, SUB, 128), vm(Y - 1, SUB, 128),
        vm(Z - 1, SUB, 128), vm(Z - 1, SUB, 128),
        vm(BLOCK, 128, dtype=F32), vm(Z, SUB, 128, dtype=F32), vm(2, SUB, 128, dtype=F32),
        dma, dma, dma, dma((Z + X - 1,)), dma, dma((2,)),
        dma, dma((24,)), dma, dma((24,)),
        dma, dma((Z,)), dma, dma((Z,)), dma, dma, dma((14,)),
        dma((4,)), dma((4,)), dma((2,)), dma((2,)),
    ]
    return pl.pallas_call(
        kernel,
        out_shape=jax.ShapeDtypeStruct((SUB, COLS), F32),
        in_specs=[pl.BlockSpec(memory_space=pl.ANY)] * 2,
        out_specs=pl.BlockSpec(memory_space=pltpu.VMEM),
        scratch_shapes=scratch,
        compiler_params=pltpu.CompilerParams(
            collective_id=0, has_side_effects=True, vmem_limit_bytes=60 * 1024 * 1024
        ),
        cost_estimate=pl.CostEstimate(
            flops=2 * CORES * TOK * Z * WIDTH * (COLS + BLOCK),
            bytes_accessed=TOK * (2 * Z * WIDTH + COLS) * 2,
            transcendentals=0,
        ),
    )(activations, out_grads)


def solution(mesh):
    return jax.shard_map(
        per_device,
        mesh=mesh,
        in_specs=(P(("narrow", "wide"), None), P(("narrow", "wide"), None)),
        out_specs=P(("narrow", "wide"), None),
        check_vma=False,
    )
```

```python
import math

import jax
import jax.numpy as jnp
from jax import lax
from jax.experimental import pallas as pl
from jax.experimental.pallas import tpu as pltpu
from jax.sharding import PartitionSpec as P

Z, CORES, X, Y = 8, 2, 4, 8
BLOCK = 128
HALF = BLOCK // 2
SUB = 16
TOK = 256
WIDTH = X * BLOCK
COLS = 512
F32, BF16 = jnp.float32, jnp.bfloat16
MESH = pl.DeviceIdType.MESH

OFFSET = (4, 3, 5, 2, 6, 1, 7, 0)
STEP = {offset: i for i, offset in enumerate(OFFSET)}
AHEAD = 3


def kernel(
    act_ref, grad_ref, out_ref,
    a_buf, g_buf, h_buf, t_buf, m_buf,
    zs, zr, ys, yr, xs0, xr0, xs1, xr1, vs0, vr0, vs, vr,
    z2s, z2r, y2s, y2r, v2s, v2r, z3s, z3r, y3s, y3r,
    z_acc, y_acc, v_acc,
    load_sem, gload_sem, asend, arecv, gsend, grecv,
    zssem, zrsem, yssem, yrsem, x0ssem, x0rsem, x1ssem, x1rsem, v0ssem, vssem, vrsem,
    s2sem, r2sem, s3sem, r3sem,
):
    n = lax.axis_index("narrow")
    w = lax.axis_index("wide")
    z, core = n // CORES, n % CORES
    x, y = w // Y, w % Y
    other = 1 - core

    def at_z(d):
        return (((z + d + Z) % Z) * CORES + core, w)

    def at_y(d):
        return (n, x * Y + (y + d + Y) % Y)

    def at_x(d):
        return (n, ((x + d + X) % X) * Y + y)

    sibling = (z * CORES + other, w)

    def remote(src, dst, ssem, rsem, target):
        return pltpu.make_async_remote_copy(
            src_ref=src, dst_ref=dst, send_sem=ssem, recv_sem=rsem,
            device_id=target, device_id_type=MESH,
        )

    def drain(buf, sem):
        pltpu.make_async_copy(buf, buf, sem).wait()

    def place(i):
        return (z + 4 + i // 2 - (i % 2) * i + 2 * Z) % Z

    def own_load(i):
        return pltpu.make_async_copy(
            act_ref.at[:, pl.ds((place(i) * CORES + core) * WIDTH, WIDTH)],
            a_buf.at[i, pl.ds(core * TOK, TOK), :],
            load_sem,
        )

    def swap(i, half):
        return remote(
            act_ref.at[:, pl.ds((place(i) * CORES + other) * WIDTH, WIDTH)],
            a_buf.at[i, pl.ds(half * TOK, TOK), :],
            asend, arecv.at[i + X - 1], sibling,
        )

    def columns(j):
        return pl.multiple_of((x + j) % X * BLOCK, BLOCK)

    def first_swap(j, half):
        return remote(
            act_ref.at[:, pl.ds((place(0) * CORES + other) * WIDTH + columns(j), BLOCK)],
            a_buf.at[0, pl.ds(half * TOK, TOK), pl.ds(columns(j), BLOCK)],
            asend, arecv.at[j], sibling,
        )

    def g_swap(part, half):
        there = pl.ds(part * (COLS // 2), COLS // 2)
        return remote(
            grad_ref.at[:, there], g_buf.at[pl.ds(half * TOK, TOK), there],
            gsend, grecv.at[part], sibling,
        )

    g_load = pltpu.make_async_copy(grad_ref, g_buf.at[pl.ds(core * TOK, TOK), :], gload_sem)

    barrier = pltpu.get_barrier_semaphore()
    pl.semaphore_signal(barrier, inc=1, device_id=sibling, device_id_type=MESH)
    for d in range(1, Z):
        pl.semaphore_signal(barrier, inc=1, device_id=at_z(d), device_id_type=MESH)
    for d in range(1, Y):
        pl.semaphore_signal(barrier, inc=1, device_id=at_y(d), device_id_type=MESH)
    for d in range(1, X):
        pl.semaphore_signal(barrier, inc=1, device_id=at_x(d), device_id_type=MESH)

    g_load.start()

    @pl.loop(0, Z)
    def _(i):
        own_load(i).start()

    row = (lax.broadcasted_iota(jnp.int32, (BLOCK, BLOCK), 0) + y * SUB) & (BLOCK - 1)
    col = lax.broadcasted_iota(jnp.int32, (BLOCK, BLOCK), 1)
    bits = row & col
    bits = bits ^ (bits >> 4)
    bits = bits ^ (bits >> 2)
    bits = bits ^ (bits >> 1)
    h_buf[...] = (1 - 2 * (bits & 1)).astype(F32).astype(BF16)

    pl.semaphore_wait(barrier, 1 + (Z - 1) + (Y - 1) + (X - 1))

    g_swap(1, core).start()
    for j in (2, 0, 1, 3):
        first_swap(j, core).start()
    g_swap(0, core).start()
    for i in range(1, AHEAD):
        swap(i, core).start()

    def turn(i, j):
        t_buf[j * BLOCK : (j + 1) * BLOCK] = lax.dot_general(
            h_buf[...],
            a_buf[i, :, pl.ds(columns(j), BLOCK)],
            (((1,), (1,)), ((), ())),
            preferred_element_type=F32,
        ).astype(BF16)

    def compute_first():
        g_load.wait()
        drain(a_buf.at[:, pl.ds(core * TOK, TOK), :], load_sem)
        g_swap(1, other).wait_recv()
        first_swap(2, other).wait_recv()
        turn(0, 2)
        m_buf[0, 2, :, 256:512] = jnp.dot(
            t_buf[2 * BLOCK : 3 * BLOCK], g_buf[:, 256:512], preferred_element_type=F32
        )

    def compute(i):
        if i == 0:
            for j in (0, 1, 3):
                first_swap(j, other).wait_recv()
            g_swap(0, other).wait_recv()
        else:
            swap(i, other).wait_recv()
        if i + AHEAD < Z:
            swap(i + AHEAD, core).start()
        for j in range(X):
            if i > 0 or j != 2:
                turn(i, j)
        m_buf[i] = jnp.dot(t_buf[...], g_buf[...], preferred_element_type=F32).reshape(X, BLOCK, COLS)

    def way_sign(way):
        return 1 - 2 * way

    def slot(way, j, k):
        if k == 0:
            return 24 + 2 * way + j % 2
        if k == 3:
            return 16 + 2 * j + way
        return 8 * (k - 1) + 4 * way + j

    def mark(way, j, k):
        return 16 + j if k == 3 else slot(way, j, k) - 4 * (k == 0)

    def z_copy(way, j, k):
        return remote(
            zs.at[slot(way, j, k)], zr.at[slot(way, j, k)], zssem, zrsem.at[mark(way, j, k)],
            at_z(way_sign(way)),
        )

    def begins(way, j):
        return j // 2 == way

    def z_step(way, j, k):
        i = STEP[(way_sign(way) * (4 - k)) % Z]
        part = m_buf[i, j, :, 0:128]
        if k >= 2 or (k == 1 and begins(way, j)):
            z_copy(way, j, k - 1).wait_recv()
            part = part + zr[slot(way, j, k - 1)].astype(F32)
        zs[slot(way, j, k)] = part.astype(BF16)
        z_copy(way, j, k).start()

    def y_copy(way, j, k):
        return remote(
            ys.at[slot(way, j, k)], yr.at[slot(way, j, k)], yssem, yrsem.at[mark(way, j, k)],
            at_y(way_sign(way)),
        )

    def y_step(way, j, k):
        first = ((way_sign(way) * (4 - k)) % Y) * SUB
        part = m_buf[:, j, first : first + SUB, 128:256]
        if k >= 2 or (k == 1 and begins(way, j)):
            y_copy(way, j, k - 1).wait_recv()
            part = part + yr[slot(way, j, k - 1)].astype(F32)
        ys[slot(way, j, k)] = part.astype(BF16)
        y_copy(way, j, k).start()

    def x0_copy(way, i):
        return remote(
            xs0.at[i, way], xr0.at[i, way], x0ssem, x0rsem.at[i],
            at_x(way_sign(way)),
        )

    def x1_copy(way, i):
        return remote(
            xs1.at[i, way], xr1.at[i, way], x1ssem, x1rsem.at[i],
            at_x(way_sign(way)),
        )

    def v_slot(way, k, h):
        return 8 + 2 * h + way if k == 3 else 4 * (k - 1) + 2 * way + h

    def v_copy(way, k, h):
        if k == 0:
            src, dst, ssem, mine = vs0.at[way, h], vr0.at[way, h], v0ssem, 10 + 2 * way + h
        else:
            at = v_slot(way, k, h)
            src, dst, ssem, mine = vs.at[at], vr.at[at], vssem, 8 + h if k == 3 else at
        return remote(src, dst, ssem, vrsem.at[mine], at_z(way_sign(way)))

    def w_copy(j, h):
        return remote(
            v2s.at[h, j - 1], v2r.at[h, j - 1], s2sem.at[2 + h], r2sem.at[2 + h], at_y(j)
        )

    def x0_step(i):
        for way in range(2):
            xs0[i, way] = m_buf[i, 2, way * HALF : (way + 1) * HALF, 256:512].astype(BF16)
            x0_copy(way, i).start()

    def x1_step(i):
        drain(xr0.at[i], x0rsem.at[i])
        for way in range(2):
            j = 1 + 2 * way
            mine = slice(way * HALF, (way + 1) * HALF)
            rest = slice((1 - way) * HALF, (2 - way) * HALF)
            xs1[i, way, mine] = (m_buf[i, j, mine, 256:512] + xr0[i, way].astype(F32)).astype(BF16)
            xs1[i, way, rest] = m_buf[i, j, rest, 256:512].astype(BF16)
            x1_copy(way, i).start()

    def x2_rows(i, rows, h):
        there = slice(h * 128, (h + 1) * 128)
        return (
            m_buf[i, 0, rows, 256 + h * 128 : 384 + h * 128]
            + xr1[i, 0, rows, there].astype(F32)
            + xr1[i, 1, rows, there].astype(F32)
        )

    def v_step(i, h):
        if i == 0:
            for way in range(2):
                rows = slice(way * HALF, (way + 1) * HALF)
                vs0[way, h] = x2_rows(0, rows, h).astype(BF16)
                v_copy(way, 0, h).start()
            return
        if i < Z - 1:
            way, k = 1 - i % 2, (i + 1) // 2
            v_copy(way, k - 1, h).wait_recv()
            if k == 1:
                mine = slice(way * HALF, (way + 1) * HALF)
                rest = slice((1 - way) * HALF, (2 - way) * HALF)
                vs[v_slot(way, 1, h), mine] = (
                    x2_rows(i, mine, h) + vr0[way, h].astype(F32)
                ).astype(BF16)
                vs[v_slot(way, 1, h), rest] = x2_rows(i, rest, h).astype(BF16)
            else:
                vs[v_slot(way, k, h)] = (
                    x2_rows(i, slice(0, BLOCK), h) + vr[v_slot(way, k - 1, h)].astype(F32)
                ).astype(BF16)
            v_copy(way, k, h).start()
            return
        drain(vr.at[pl.ds(8 + 2 * h, 2)], vrsem.at[8 + h])
        part = (
            x2_rows(i, slice(0, BLOCK), h) + vr[8 + 2 * h].astype(F32) + vr[9 + 2 * h].astype(F32)
        )
        v_acc[h] = part[0:SUB]
        for j in OFFSET[:-1]:
            v2s[h, j - 1] = part[j * SUB : (j + 1) * SUB].astype(BF16)
            w_copy(j, h).start()

    def x1_arrived(i):
        drain(xr1.at[i], x1rsem.at[i])

    def z2_step(j):
        drain(zr.at[pl.ds(slot(0, j, 3), 2)], zrsem.at[mark(0, j, 3)])
        part = m_buf[Z - 1, j, :, 0:128] + zr[slot(0, j, 3)].astype(F32) + zr[slot(1, j, 3)].astype(F32)
        if j == 0:
            z_acc[...] = part
        else:
            z2s[j - 1] = part.astype(BF16)
            remote(z2s.at[j - 1], z2r.at[j - 1], s2sem.at[0], r2sem.at[0], at_x(j)).start()

    def y2_step(j):
        drain(yr.at[pl.ds(slot(0, j, 3), 2)], yrsem.at[mark(0, j, 3)])
        part = m_buf[:, j, 0:SUB, 128:256] + yr[slot(0, j, 3)].astype(F32) + yr[slot(1, j, 3)].astype(F32)
        if j == 0:
            y_acc[...] = part
        else:
            y2s[j - 1] = part.astype(BF16)
            remote(y2s.at[j - 1], y2r.at[j - 1], s2sem.at[1], r2sem.at[1], at_x(j)).start()

    def z3_step():
        drain(z2r, r2sem.at[0])
        part = z_acc[...]
        for q in range(X - 1):
            part = part + z2r[q].astype(F32)
        z_acc[...] = part
        for j in OFFSET[:-1]:
            z3s[j - 1] = part[j * SUB : (j + 1) * SUB].astype(BF16)
            remote(z3s.at[j - 1], z3r.at[j - 1], s3sem.at[0], r3sem.at[0], at_y(j)).start()

    def y3_step():
        drain(y2r, r2sem.at[1])
        part = y_acc[...]
        for q in range(X - 1):
            part = part + y2r[q].astype(F32)
        y_acc[...] = part
        for j in OFFSET[:-1]:
            y3s[j - 1] = part[STEP[j]].astype(BF16)
            remote(y3s.at[j - 1], y3r.at[j - 1], s3sem.at[1], r3sem.at[1], at_z(j)).start()

    scale = 1.0 / (Z * CORES * X * Y * math.sqrt(BLOCK))

    def finish(own, received, sem, first):
        drain(received, sem)
        total = own
        for q in range(received.shape[0]):
            total = total + received[q].astype(F32)
        out_ref[:, first : first + 128] = total * scale


    compute_first()
    x0_step(0)
    compute(0)
    compute(1)
    x0_step(1)
    compute(2)
    x0_step(2)
    z_step(1, 2, 0)
    compute(3)
    x0_step(3)
    z_step(0, 1, 0)
    compute(4)
    x0_step(4)
    z_step(1, 3, 0)
    x1_step(0)
    compute(5)
    compute(6)
    compute(7)
    y_step(1, 2, 0)
    x0_step(6)
    z_step(0, 0, 0)
    y_step(0, 1, 0)
    z_step(1, 1, 1)
    y_step(1, 3, 0)
    x1_step(2)
    z_step(0, 2, 1)
    y_step(1, 1, 1)
    z_step(1, 2, 1)
    y_step(0, 0, 0)
    z_step(1, 0, 1)
    y_step(0, 2, 1)
    z_step(0, 1, 1)
    y_step(1, 0, 1)
    z_step(1, 3, 1)
    x1_step(1)
    x0_step(5)
    z_step(0, 3, 1)
    y_step(0, 3, 1)
    x1_step(4)
    x1_arrived(0)
    v_step(0, 1)
    v_step(0, 0)
    x0_step(7)
    y_step(1, 2, 1)
    z_step(0, 0, 1)
    z_step(1, 1, 2)
    y_step(0, 1, 1)
    y_step(1, 3, 1)
    z_step(0, 2, 2)
    z_step(1, 2, 2)
    x1_step(3)
    y_step(1, 1, 2)
    z_step(0, 1, 2)
    z_step(1, 0, 2)
    y_step(0, 0, 1)
    y_step(0, 2, 2)
    z_step(0, 3, 2)
    x1_step(6)
    z_step(1, 3, 2)
    y_step(1, 0, 2)
    x1_arrived(2)
    v_step(2, 1)
    x1_arrived(1)
    v_step(1, 0)
    y_step(1, 2, 2)
    v_step(1, 1)
    v_step(2, 0)
    x1_step(5)
    y_step(0, 3, 2)
    y_step(1, 3, 2)
    z_step(0, 2, 3)
    y_step(0, 1, 2)
    z_step(1, 2, 3)
    z_step(0, 1, 3)
    z_step(1, 1, 3)
    y_step(1, 1, 3)
    y_step(0, 0, 2)
    z_step(0, 0, 2)
    z_step(0, 3, 3)
    z_step(1, 3, 3)
    y_step(0, 2, 3)
    x1_step(7)
    x1_arrived(4)
    v_step(4, 1)
    y_step(1, 2, 3)
    x1_arrived(3)
    v_step(3, 1)
    v_step(3, 0)
    y_step(0, 3, 3)
    v_step(4, 0)
    y_step(1, 3, 3)
    y_step(1, 0, 3)
    y_step(0, 1, 3)
    z2_step(2)
    z2_step(1)
    z_step(1, 0, 3)
    y_step(0, 0, 3)
    z_step(0, 0, 3)
    z2_step(3)
    x1_arrived(6)
    v_step(6, 1)
    y2_step(2)
    x1_arrived(5)
    v_step(5, 1)
    v_step(6, 0)
    y2_step(3)
    v_step(5, 0)
    y2_step(1)
    y2_step(0)
    z2_step(0)
    z3_step()
    x1_arrived(7)
    v_step(7, 1)
    v_step(7, 0)
    y3_step()
    finish(v_acc[1], v2r.at[1], r2sem.at[3], 384)
    finish(z_acc[0:SUB], z3r, r3sem.at[0], 0)
    finish(v_acc[0], v2r.at[0], r2sem.at[2], 256)
    finish(y_acc[Z - 1], y3r, r3sem.at[1], 128)

    drain(g_buf.at[pl.ds(0, TOK), :], gsend)

    drain(a_buf.at[:, pl.ds(0, TOK), :], asend)
    for buf, sem in (
        (zs, zssem), (ys, yssem), (xs0, x0ssem), (xs1, x1ssem), (vs0, v0ssem), (vs, vssem)
    ):
        drain(buf, sem)
    for at, buf in enumerate((z2s, y2s, v2s.at[0], v2s.at[1])):
        drain(buf, s2sem.at[at])
    for at, buf in enumerate((z3s, y3s)):
        drain(buf, s3sem.at[at])


def per_device(activations, out_grads):
    def vm(*shape, dtype=BF16):
        return pltpu.VMEM(shape, dtype)

    dma = pltpu.SemaphoreType.DMA
    scratch = [
        vm(Z, CORES * TOK, WIDTH), vm(CORES * TOK, COLS), vm(BLOCK, BLOCK), vm(WIDTH, CORES * TOK),
        vm(Z, X, BLOCK, COLS, dtype=F32),
        vm(28, BLOCK, 128), vm(28, BLOCK, 128),
        vm(28, Z, SUB, 128), vm(28, Z, SUB, 128),
        vm(Z, 2, HALF, 256), vm(Z, 2, HALF, 256),
        vm(Z, 2, BLOCK, 256), vm(Z, 2, BLOCK, 256),
        vm(2, 2, HALF, 128), vm(2, 2, HALF, 128),
        vm(12, BLOCK, 128), vm(12, BLOCK, 128),
        vm(X - 1, BLOCK, 128), vm(X - 1, BLOCK, 128),
        vm(X - 1, Z, SUB, 128), vm(X - 1, Z, SUB, 128),
        vm(2, Y - 1, SUB, 128), vm(2, Y - 1, SUB, 128),
        vm(Y - 1, SUB, 128), vm(Y - 1, SUB, 128),
        vm(Z - 1, SUB, 128), vm(Z - 1, SUB, 128),
        vm(BLOCK, 128, dtype=F32), vm(Z, SUB, 128, dtype=F32), vm(2, SUB, 128, dtype=F32),
        dma, dma, dma, dma((Z + X - 1,)), dma, dma((2,)),
        dma, dma((24,)), dma, dma((24,)),
        dma, dma((Z,)), dma, dma((Z,)), dma, dma, dma((14,)),
        dma((4,)), dma((4,)), dma((2,)), dma((2,)),
    ]
    return pl.pallas_call(
        kernel,
        out_shape=pltpu.VMEM((SUB, COLS), F32),
        in_specs=[pl.BlockSpec(memory_space=pl.ANY)] * 2,
        out_specs=pl.BlockSpec(memory_space=pltpu.VMEM),
        scratch_shapes=scratch,
        compiler_params=pltpu.CompilerParams(
            collective_id=0, has_side_effects=True, vmem_limit_bytes=56 * 1024 * 1024
        ),
        cost_estimate=pl.CostEstimate(
            flops=2 * CORES * TOK * Z * WIDTH * (COLS + BLOCK),
            bytes_accessed=TOK * (2 * Z * WIDTH + COLS) * 2,
            transcendentals=0,
        ),
    )(activations, out_grads)


def solution(mesh):
    return jax.shard_map(
        per_device,
        mesh=mesh,
        in_specs=(P(("narrow", "wide"), None), P(("narrow", "wide"), None)),
        out_specs=P(("narrow", "wide"), None),
        check_vma=False,
    )
```

```python
import math

import jax
import jax.numpy as jnp
from jax import lax
from jax.experimental import pallas as pl
from jax.experimental.pallas import tpu as pltpu
from jax.sharding import PartitionSpec as P

Z, CORES, X, Y = 8, 2, 4, 8
BLOCK = 128
HALF = BLOCK // 2
SUB = 16
TOK = 256
WIDTH = X * BLOCK
COLS = 512
F32, BF16 = jnp.float32, jnp.bfloat16
MESH = pl.DeviceIdType.MESH

OFFSET = (4, 3, 5, 2, 6, 1, 7, 0)
STEP = {offset: i for i, offset in enumerate(OFFSET)}
AHEAD = 3


def kernel(
    act_ref, grad_ref, out_ref,
    a_buf, g_buf, h_buf, t_buf, m_buf,
    zs, zr, ys, yr, xs0, xr0, xs1, xr1, vs0, vr0, vs, vr,
    z2s, z2r, y2s, y2r, v2s, v2r, z3s, z3r, y3s, y3r,
    z_acc, y_acc, v_acc,
    load_sem, gload_sem, asend, arecv, gsend, grecv,
    zssem, zrsem, yssem, yrsem, x0ssem, x0rsem, x1ssem, x1rsem, v0ssem, vssem, vrsem,
    s2sem, r2sem, s3sem, r3sem,
):
    n = lax.axis_index("narrow")
    w = lax.axis_index("wide")
    z, core = n // CORES, n % CORES
    x, y = w // Y, w % Y
    other = 1 - core

    def at_z(d):
        return (((z + d + Z) % Z) * CORES + core, w)

    def at_y(d):
        return (n, x * Y + (y + d + Y) % Y)

    def at_x(d):
        return (n, ((x + d + X) % X) * Y + y)

    sibling = (z * CORES + other, w)

    def remote(src, dst, ssem, rsem, target):
        return pltpu.make_async_remote_copy(
            src_ref=src, dst_ref=dst, send_sem=ssem, recv_sem=rsem,
            device_id=target, device_id_type=MESH,
        )

    def drain(buf, sem):
        pltpu.make_async_copy(buf, buf, sem).wait()

    def place(i):
        return (z + 4 + i // 2 - (i % 2) * i + 2 * Z) % Z

    def own_load(i):
        return pltpu.make_async_copy(
            act_ref.at[:, pl.ds((place(i) * CORES + core) * WIDTH, WIDTH)],
            a_buf.at[i, pl.ds(core * TOK, TOK), :],
            load_sem,
        )

    def swap(i, half):
        return remote(
            act_ref.at[:, pl.ds((place(i) * CORES + other) * WIDTH, WIDTH)],
            a_buf.at[i, pl.ds(half * TOK, TOK), :],
            asend, arecv.at[i + X - 1], sibling,
        )

    def columns(j):
        return pl.multiple_of((x + j) % X * BLOCK, BLOCK)

    def first_swap(j, half):
        return remote(
            act_ref.at[:, pl.ds((place(0) * CORES + other) * WIDTH + columns(j), BLOCK)],
            a_buf.at[0, pl.ds(half * TOK, TOK), pl.ds(columns(j), BLOCK)],
            asend, arecv.at[j], sibling,
        )

    def g_swap(part, half):
        there = pl.ds(part * (COLS // 2), COLS // 2)
        return remote(
            grad_ref.at[:, there], g_buf.at[pl.ds(half * TOK, TOK), there],
            gsend, grecv.at[part], sibling,
        )

    g_load = pltpu.make_async_copy(grad_ref, g_buf.at[pl.ds(core * TOK, TOK), :], gload_sem)

    barrier = pltpu.get_barrier_semaphore()
    pl.semaphore_signal(barrier, inc=1, device_id=sibling, device_id_type=MESH)
    for d in range(1, Z):
        pl.semaphore_signal(barrier, inc=1, device_id=at_z(d), device_id_type=MESH)
    for d in range(1, Y):
        pl.semaphore_signal(barrier, inc=1, device_id=at_y(d), device_id_type=MESH)
    for d in range(1, X):
        pl.semaphore_signal(barrier, inc=1, device_id=at_x(d), device_id_type=MESH)

    g_load.start()

    @pl.loop(0, Z)
    def _(i):
        own_load(i).start()

    row = (lax.broadcasted_iota(jnp.int32, (BLOCK, BLOCK), 0) + y * SUB) & (BLOCK - 1)
    col = lax.broadcasted_iota(jnp.int32, (BLOCK, BLOCK), 1)
    bits = row & col
    bits = bits ^ (bits >> 4)
    bits = bits ^ (bits >> 2)
    bits = bits ^ (bits >> 1)
    h_buf[...] = (1 - 2 * (bits & 1)).astype(F32).astype(BF16)

    pl.semaphore_wait(barrier, 1 + (Z - 1) + (Y - 1) + (X - 1))

    g_swap(1, core).start()
    for j in (2, 0, 1, 3):
        first_swap(j, core).start()
    g_swap(0, core).start()
    for i in range(1, AHEAD):
        swap(i, core).start()

    def turn(i, j):
        t_buf[j * BLOCK : (j + 1) * BLOCK] = lax.dot_general(
            h_buf[...],
            a_buf[i, :, pl.ds(columns(j), BLOCK)],
            (((1,), (1,)), ((), ())),
            preferred_element_type=F32,
        ).astype(BF16)

    def compute_first():
        g_load.wait()
        drain(a_buf.at[:, pl.ds(core * TOK, TOK), :], load_sem)
        g_swap(1, other).wait_recv()
        first_swap(2, other).wait_recv()
        turn(0, 2)
        m_buf[0, 2, :, 256:512] = jnp.dot(
            t_buf[2 * BLOCK : 3 * BLOCK], g_buf[:, 256:512], preferred_element_type=F32
        )

    def compute(i):
        if i == 0:
            for j in (0, 1, 3):
                first_swap(j, other).wait_recv()
            g_swap(0, other).wait_recv()
        else:
            swap(i, other).wait_recv()
        if i + AHEAD < Z:
            swap(i + AHEAD, core).start()
        for j in range(X):
            if i > 0 or j != 2:
                turn(i, j)
        m_buf[i] = jnp.dot(t_buf[...], g_buf[...], preferred_element_type=F32).reshape(X, BLOCK, COLS)

    def way_sign(way):
        return 1 - 2 * way

    def slot(way, j, k):
        if k == 0:
            return 24 + 2 * way + j % 2
        if k == 3:
            return 16 + 2 * j + way
        return 8 * (k - 1) + 4 * way + j

    def mark(way, j, k):
        return 16 + j if k == 3 else slot(way, j, k) - 4 * (k == 0)

    def z_copy(way, j, k):
        return remote(
            zs.at[slot(way, j, k)], zr.at[slot(way, j, k)], zssem, zrsem.at[mark(way, j, k)],
            at_z(way_sign(way)),
        )

    def begins(way, j):
        return j // 2 == way

    def z_step(way, j, k):
        i = STEP[(way_sign(way) * (4 - k)) % Z]
        part = m_buf[i, j, :, 0:128]
        if k >= 2 or (k == 1 and begins(way, j)):
            z_copy(way, j, k - 1).wait_recv()
            part = part + zr[slot(way, j, k - 1)].astype(F32)
        zs[slot(way, j, k)] = part.astype(BF16)
        z_copy(way, j, k).start()

    def y_copy(way, j, k):
        return remote(
            ys.at[slot(way, j, k)], yr.at[slot(way, j, k)], yssem, yrsem.at[mark(way, j, k)],
            at_y(way_sign(way)),
        )

    def y_step(way, j, k):
        first = ((way_sign(way) * (4 - k)) % Y) * SUB
        part = m_buf[:, j, first : first + SUB, 128:256]
        if k >= 2 or (k == 1 and begins(way, j)):
            y_copy(way, j, k - 1).wait_recv()
            part = part + yr[slot(way, j, k - 1)].astype(F32)
        ys[slot(way, j, k)] = part.astype(BF16)
        y_copy(way, j, k).start()

    def x0_copy(way, i):
        return remote(
            xs0.at[i, way], xr0.at[i, way], x0ssem, x0rsem.at[i],
            at_x(way_sign(way)),
        )

    def x1_copy(way, i, h):
        return remote(
            xs1.at[i, h, way], xr1.at[i, h, way], x1ssem, x1rsem.at[i, h],
            at_x(way_sign(way)),
        )

    def v_slot(way, k, h):
        return 8 + 2 * h + way if k == 3 else 4 * (k - 1) + 2 * way + h

    def v_copy(way, k, h):
        if k == 0:
            src, dst, ssem, mine = vs0.at[way, h], vr0.at[way, h], v0ssem, 10 + 2 * way + h
        else:
            at = v_slot(way, k, h)
            src, dst, ssem, mine = vs.at[at], vr.at[at], vssem, 8 + h if k == 3 else at
        return remote(src, dst, ssem, vrsem.at[mine], at_z(way_sign(way)))

    def w_copy(j, h):
        return remote(
            v2s.at[h, j - 1], v2r.at[h, j - 1], s2sem.at[2 + h], r2sem.at[2 + h], at_y(j)
        )

    def x0_step(i):
        for way in range(2):
            xs0[i, way] = m_buf[i, 2, way * HALF : (way + 1) * HALF, 256:512].astype(BF16)
            x0_copy(way, i).start()

    def x1_step(i):
        drain(xr0.at[i], x0rsem.at[i])
        for h in range(2):
            there = slice(256 + h * 128, 384 + h * 128)
            for way in range(2):
                j = 1 + 2 * way
                mine = slice(way * HALF, (way + 1) * HALF)
                rest = slice((1 - way) * HALF, (2 - way) * HALF)
                came = xr0[i, way, :, h * 128 : (h + 1) * 128].astype(F32)
                xs1[i, h, way, mine] = (m_buf[i, j, mine, there] + came).astype(BF16)
                xs1[i, h, way, rest] = m_buf[i, j, rest, there].astype(BF16)
                x1_copy(way, i, h).start()

    def x2_rows(i, rows, h):
        return (
            m_buf[i, 0, rows, 256 + h * 128 : 384 + h * 128]
            + xr1[i, h, 0, rows].astype(F32)
            + xr1[i, h, 1, rows].astype(F32)
        )

    def v_step(i, h):
        drain(xr1.at[i, h], x1rsem.at[i, h])
        if i == 0:
            for way in range(2):
                rows = slice(way * HALF, (way + 1) * HALF)
                vs0[way, h] = x2_rows(0, rows, h).astype(BF16)
                v_copy(way, 0, h).start()
            return
        if i < Z - 1:
            way, k = 1 - i % 2, (i + 1) // 2
            v_copy(way, k - 1, h).wait_recv()
            if k == 1:
                mine = slice(way * HALF, (way + 1) * HALF)
                rest = slice((1 - way) * HALF, (2 - way) * HALF)
                vs[v_slot(way, 1, h), mine] = (
                    x2_rows(i, mine, h) + vr0[way, h].astype(F32)
                ).astype(BF16)
                vs[v_slot(way, 1, h), rest] = x2_rows(i, rest, h).astype(BF16)
            else:
                vs[v_slot(way, k, h)] = (
                    x2_rows(i, slice(0, BLOCK), h) + vr[v_slot(way, k - 1, h)].astype(F32)
                ).astype(BF16)
            v_copy(way, k, h).start()
            return
        drain(vr.at[pl.ds(8 + 2 * h, 2)], vrsem.at[8 + h])
        part = (
            x2_rows(i, slice(0, BLOCK), h) + vr[8 + 2 * h].astype(F32) + vr[9 + 2 * h].astype(F32)
        )
        v_acc[h] = part[0:SUB]
        for j in OFFSET[:-1]:
            v2s[h, j - 1] = part[j * SUB : (j + 1) * SUB].astype(BF16)
            w_copy(j, h).start()

    def z2_step(j):
        drain(zr.at[pl.ds(slot(0, j, 3), 2)], zrsem.at[mark(0, j, 3)])
        part = m_buf[Z - 1, j, :, 0:128] + zr[slot(0, j, 3)].astype(F32) + zr[slot(1, j, 3)].astype(F32)
        if j == 0:
            z_acc[...] = part
        else:
            z2s[j - 1] = part.astype(BF16)
            remote(z2s.at[j - 1], z2r.at[j - 1], s2sem.at[0], r2sem.at[0], at_x(j)).start()

    def y2_step(j):
        drain(yr.at[pl.ds(slot(0, j, 3), 2)], yrsem.at[mark(0, j, 3)])
        part = m_buf[:, j, 0:SUB, 128:256] + yr[slot(0, j, 3)].astype(F32) + yr[slot(1, j, 3)].astype(F32)
        if j == 0:
            y_acc[...] = part
        else:
            y2s[j - 1] = part.astype(BF16)
            remote(y2s.at[j - 1], y2r.at[j - 1], s2sem.at[1], r2sem.at[1], at_x(j)).start()

    def z3_step():
        drain(z2r, r2sem.at[0])
        part = z_acc[...]
        for q in range(X - 1):
            part = part + z2r[q].astype(F32)
        z_acc[...] = part
        for j in OFFSET[:-1]:
            z3s[j - 1] = part[j * SUB : (j + 1) * SUB].astype(BF16)
            remote(z3s.at[j - 1], z3r.at[j - 1], s3sem.at[0], r3sem.at[0], at_y(j)).start()

    def y3_step():
        drain(y2r, r2sem.at[1])
        part = y_acc[...]
        for q in range(X - 1):
            part = part + y2r[q].astype(F32)
        y_acc[...] = part
        for j in OFFSET[:-1]:
            y3s[j - 1] = part[STEP[j]].astype(BF16)
            remote(y3s.at[j - 1], y3r.at[j - 1], s3sem.at[1], r3sem.at[1], at_z(j)).start()

    scale = 1.0 / (Z * CORES * X * Y * math.sqrt(BLOCK))

    def finish(own, received, sem, first):
        drain(received, sem)
        total = own
        for q in range(received.shape[0]):
            total = total + received[q].astype(F32)
        out_ref[:, first : first + 128] = total * scale


    compute_first()
    x0_step(0)
    compute(0)
    compute(1)
    x0_step(1)
    compute(2)
    x0_step(2)
    z_step(1, 2, 0)
    compute(3)
    x0_step(3)
    z_step(0, 1, 0)
    compute(4)
    x0_step(4)
    z_step(1, 3, 0)
    x1_step(0)
    compute(5)
    compute(6)
    compute(7)
    y_step(1, 2, 0)
    x0_step(6)
    z_step(0, 0, 0)
    y_step(0, 1, 0)
    z_step(1, 1, 1)
    y_step(1, 3, 0)
    x1_step(2)
    z_step(0, 2, 1)
    y_step(1, 1, 1)
    z_step(1, 2, 1)
    y_step(0, 0, 0)
    z_step(1, 0, 1)
    y_step(0, 2, 1)
    z_step(0, 1, 1)
    y_step(1, 0, 1)
    z_step(1, 3, 1)
    x1_step(1)
    x0_step(5)
    z_step(0, 3, 1)
    y_step(0, 3, 1)
    x1_step(4)
    v_step(0, 1)
    v_step(0, 0)
    x0_step(7)
    y_step(1, 2, 1)
    z_step(0, 0, 1)
    z_step(1, 1, 2)
    y_step(0, 1, 1)
    y_step(1, 3, 1)
    z_step(0, 2, 2)
    z_step(1, 2, 2)
    x1_step(3)
    y_step(1, 1, 2)
    z_step(0, 1, 2)
    z_step(1, 0, 2)
    y_step(0, 0, 1)
    y_step(0, 2, 2)
    z_step(0, 3, 2)
    x1_step(6)
    z_step(1, 3, 2)
    y_step(1, 0, 2)
    v_step(2, 1)
    v_step(1, 0)
    y_step(1, 2, 2)
    v_step(1, 1)
    v_step(2, 0)
    x1_step(5)
    y_step(0, 3, 2)
    y_step(1, 3, 2)
    z_step(0, 2, 3)
    y_step(0, 1, 2)
    z_step(1, 2, 3)
    z_step(0, 1, 3)
    z_step(1, 1, 3)
    y_step(1, 1, 3)
    y_step(0, 0, 2)
    z_step(0, 0, 2)
    z_step(0, 3, 3)
    z_step(1, 3, 3)
    y_step(0, 2, 3)
    x1_step(7)
    v_step(4, 1)
    y_step(1, 2, 3)
    v_step(3, 1)
    v_step(3, 0)
    y_step(0, 3, 3)
    v_step(4, 0)
    y_step(1, 3, 3)
    y_step(1, 0, 3)
    y_step(0, 1, 3)
    z2_step(2)
    z2_step(1)
    z_step(1, 0, 3)
    y_step(0, 0, 3)
    z_step(0, 0, 3)
    z2_step(3)
    v_step(6, 1)
    y2_step(2)
    v_step(5, 1)
    v_step(6, 0)
    y2_step(3)
    v_step(5, 0)
    y2_step(1)
    y2_step(0)
    z2_step(0)
    z3_step()
    v_step(7, 1)
    v_step(7, 0)
    y3_step()
    finish(v_acc[1], v2r.at[1], r2sem.at[3], 384)
    finish(z_acc[0:SUB], z3r, r3sem.at[0], 0)
    finish(v_acc[0], v2r.at[0], r2sem.at[2], 256)
    finish(y_acc[Z - 1], y3r, r3sem.at[1], 128)

    drain(g_buf.at[pl.ds(0, TOK), :], gsend)

    drain(a_buf.at[:, pl.ds(0, TOK), :], asend)
    for buf, sem in (
        (zs, zssem), (ys, yssem), (xs0, x0ssem), (xs1, x1ssem), (vs0, v0ssem), (vs, vssem)
    ):
        drain(buf, sem)
    for at, buf in enumerate((z2s, y2s, v2s.at[0], v2s.at[1])):
        drain(buf, s2sem.at[at])
    for at, buf in enumerate((z3s, y3s)):
        drain(buf, s3sem.at[at])


def per_device(activations, out_grads):
    def vm(*shape, dtype=BF16):
        return pltpu.VMEM(shape, dtype)

    dma = pltpu.SemaphoreType.DMA
    scratch = [
        vm(Z, CORES * TOK, WIDTH), vm(CORES * TOK, COLS), vm(BLOCK, BLOCK), vm(WIDTH, CORES * TOK),
        vm(Z, X, BLOCK, COLS, dtype=F32),
        vm(28, BLOCK, 128), vm(28, BLOCK, 128),
        vm(28, Z, SUB, 128), vm(28, Z, SUB, 128),
        vm(Z, 2, HALF, 256), vm(Z, 2, HALF, 256),
        vm(Z, 2, 2, BLOCK, 128), vm(Z, 2, 2, BLOCK, 128),
        vm(2, 2, HALF, 128), vm(2, 2, HALF, 128),
        vm(12, BLOCK, 128), vm(12, BLOCK, 128),
        vm(X - 1, BLOCK, 128), vm(X - 1, BLOCK, 128),
        vm(X - 1, Z, SUB, 128), vm(X - 1, Z, SUB, 128),
        vm(2, Y - 1, SUB, 128), vm(2, Y - 1, SUB, 128),
        vm(Y - 1, SUB, 128), vm(Y - 1, SUB, 128),
        vm(Z - 1, SUB, 128), vm(Z - 1, SUB, 128),
        vm(BLOCK, 128, dtype=F32), vm(Z, SUB, 128, dtype=F32), vm(2, SUB, 128, dtype=F32),
        dma, dma, dma, dma((Z + X - 1,)), dma, dma((2,)),
        dma, dma((24,)), dma, dma((24,)),
        dma, dma((Z,)), dma, dma((Z, 2)), dma, dma, dma((14,)),
        dma((4,)), dma((4,)), dma((2,)), dma((2,)),
    ]
    return pl.pallas_call(
        kernel,
        out_shape=pltpu.VMEM((SUB, COLS), F32),
        in_specs=[pl.BlockSpec(memory_space=pl.ANY)] * 2,
        out_specs=pl.BlockSpec(memory_space=pltpu.VMEM),
        scratch_shapes=scratch,
        compiler_params=pltpu.CompilerParams(
            collective_id=0, has_side_effects=True, vmem_limit_bytes=56 * 1024 * 1024
        ),
        cost_estimate=pl.CostEstimate(
            flops=2 * CORES * TOK * Z * WIDTH * (COLS + BLOCK),
            bytes_accessed=TOK * (2 * Z * WIDTH + COLS) * 2,
            transcendentals=0,
        ),
    )(activations, out_grads)


def solution(mesh):
    return jax.shard_map(
        per_device,
        mesh=mesh,
        in_specs=(P(("narrow", "wide"), None), P(("narrow", "wide"), None)),
        out_specs=P(("narrow", "wide"), None),
        check_vma=False,
    )
```
